32 devices in a mesh: gz: 4 (over x, core), gx: 8 (over z, y).
Axes of the slice: x: 2, y: 2, z: 4, core: 2. Of those that a mesh axis runs over, the one named last changes fastest.
Arguments:
- state: float32 [6, 64, 2048], P(None, 'gz', 'gx'), may hold values from -5 to 5, as said below
- state_cot: float32 [6, 64, 2048], P(None, 'gz', 'gx'), may hold values from -6 to 6
- w_in: bfloat16 [128, 12], replicated, may hold values from -1.75 to 1.75
- w_mid: bfloat16 [128, 128], replicated, may hold values from -0.5 to 0.5
- w_out: bfloat16 [6, 128], replicated, may hold values from -0.5 to 0.5
- radiation: float32 [64, 64], replicated, may hold values from -0.75 to 0.75
- fall_rate: float32 [2048], P('gx'), may hold values from 20 to 2000
- active: int32 [2048], P('gx'), may hold values 0 or 1
Outputs:
- new_state: float32 [6, 64, 2048], P(None, 'gz', 'gx')
- state_grad: float32 [6, 64, 2048], P(None, 'gz', 'gx')
- grad_in: float32 [128, 12], replicated
- grad_mid: float32 [128, 128], replicated
- grad_out: float32 [6, 128], replicated
The draws below stay inside these ranges and needn't reach their ends.
Inputs may be any that keep to these rules, and one draw needn't show every extreme that they name: `state`: fields come in the order u, v, w, theta, total water, rain water; rain water lies between 0.05 and 1.
All inputs are finite; a program needn't handle non-finite values. No bound on the sum of `active` on one device may be relied on, other than what follows from the above.
Results may differ from the reference program's by a relative error of at most 0.00045.
The reference program's roundings to bfloat16 on the way (of `features`) count: a program that leaves them out, or rounds other values in their place, can miss the bound.
Values sent between devices are 32-bit elements; how exact they have to be, the bound alone decides.
A program may use at most 64 MiB of HBM per device.

```python
import math
import jax
import jax.numpy as jnp
from jax import lax

NFIELD = 6
HID = 128
NY = 64
NX = 32
NZ = 64
NCOL = 2048


def draw_state(key, part):
    subkeys = jax.random.split(jax.random.fold_in(key, 17), 3)
    scales = jnp.array([1.0, 1.0, 0.5, 1.0, 1.0], jnp.float32)[:, None, None]
    moving = jnp.clip(jax.random.normal(subkeys[1], (5, NZ, NCOL), jnp.float32), -4.0, 4.0) * scales
    rain_water = jnp.exp(jax.random.uniform(subkeys[2], (NZ, NCOL), jnp.float32, math.log(0.05), 0.0))
    return jnp.concatenate([moving, rain_water[None]], 0)


def set_ends(drawn, own_key, smallest, top_value):
    dims = drawn.shape
    index_at = [jax.random.randint(jax.random.fold_in(own_key, axis), (), 0, dims[axis]) for axis in range(len(dims))]
    drawn = drawn.at[tuple(index_at)].set(smallest)
    longest = dims.index(max(dims))
    index_at[longest] = (index_at[longest] + 1) % dims[longest]
    return drawn.at[tuple(index_at)].set(top_value)


def steps_of(rng, dims, cuts, low, high):
    gain = 1.0
    for dim, blocks in cuts:
        draws = jax.random.uniform(jax.random.fold_in(jax.random.fold_in(rng, 6), dim), (blocks,), jnp.float32, low / len(cuts), high / len(cuts))
        gain = gain * jnp.repeat(jnp.exp(draws), dims[dim] // blocks).reshape((-1,) + (1,) * (len(dims) - 1 - dim))
    return gain


def scatter_about(key, shape, deviation, reach, shards=(), kind=jnp.bfloat16):
    gain = steps_of(key, shape, shards, -0.22, 0.18) if shards else 1.0
    entries = jax.random.normal(key, shape, jnp.float32) * deviation * gain
    return jnp.minimum(jnp.maximum(entries, -reach), reach).astype(kind)


def setup_inputs(seed: int = 0) -> dict:
    key_list = jax.random.split(jax.random.key(seed), 9)
    state = draw_state(jax.random.fold_in(key_list[8], 71), 0)
    state_cot = scatter_about(key_list[1], (NFIELD, NZ, NCOL), 1.0, 6.0, ((1, 4), (2, 8)), jnp.float32)
    w_in = scatter_about(key_list[2], (HID, 2 * NFIELD), (2 * NFIELD) ** -0.5, 1.75)
    w_mid = scatter_about(key_list[3], (HID, HID), HID ** -0.5, 0.5)
    w_out = scatter_about(key_list[4], (NFIELD, HID), HID ** -0.5, 0.5)
    radiation = scatter_about(key_list[5], (NZ, NZ), NZ ** -0.5, 0.75, (), jnp.float32)
    fall_rate = jnp.clip(jnp.exp(math.log(2000.0) - 4.6051702 * jax.random.uniform(key_list[6], (NCOL,), jnp.float32) ** steps_of(key_list[6], (NCOL,), ((0, 8),), -0.2, 0.2)), 20.0, 2000.0)
    active = set_ends((jax.random.randint(key_list[7], (NCOL,), 0, 2) < 1).astype(jnp.int32), jax.random.fold_in(key_list[7], 1), 0, 1)
    return dict(state=state, state_cot=state_cot, w_in=w_in, w_mid=w_mid, w_out=w_out, radiation=radiation, fall_rate=fall_rate, active=active)


DIFFUSION = 0.1
TIME_STEP = 0.25
CLOSURE_GAIN = 1.0
HEATING_GAIN = 1.0
FALL_GAIN = 1.0

def contract(left, right, left_dim, right_dim):
    return lax.dot_general(left, right, (((left_dim,), (right_dim,)), ((), ())), preferred_element_type=jnp.float32)

def mlp_forward(features, w_in, w_mid, w_out):
    hidden_one = jnp.tanh(jnp.dot(w_in, features, preferred_element_type=jnp.float32)).astype(jnp.bfloat16)
    hidden_two = jnp.tanh(jnp.dot(w_mid, hidden_one, preferred_element_type=jnp.float32)).astype(jnp.bfloat16)
    return jnp.dot(w_out, hidden_two, preferred_element_type=jnp.float32)

def mlp_backward(features, out_cot, w_in, w_mid, w_out):
    tanh_one = jnp.tanh(jnp.dot(w_in, features, preferred_element_type=jnp.float32))
    hidden_one = tanh_one.astype(jnp.bfloat16)
    tanh_two = jnp.tanh(jnp.dot(w_mid, hidden_one, preferred_element_type=jnp.float32))
    hidden_two = tanh_two.astype(jnp.bfloat16)
    term_out = contract(out_cot, hidden_two, 1, 1)
    pre_two = (contract(w_out, out_cot, 0, 0) * (1.0 - tanh_two * tanh_two)).astype(jnp.bfloat16)
    term_mid = contract(pre_two, hidden_one, 1, 1)
    pre_one = (contract(w_mid, pre_two, 0, 0) * (1.0 - tanh_one * tanh_one)).astype(jnp.bfloat16)
    term_in = contract(pre_one, features, 1, 1)
    feature_cot = contract(w_in, pre_one, 0, 0)
    return (feature_cot, (term_in, term_mid, term_out))

def dynamics(fields):

    def along_x(offset):
        return jnp.roll(fields, -offset, axis=2)

    def along_y(offset):
        return jnp.roll(fields, -offset, axis=3)
    x_plus, x_minus = (along_x(1), along_x(-1))
    y_plus, y_minus = (along_y(1), along_y(-1))
    deriv_x = (8.0 * (x_plus - x_minus) - (along_x(2) - along_x(-2))) / 12.0
    deriv_y = (y_plus - y_minus) / 2.0
    laplace = x_plus + x_minus + y_plus + y_minus - 4.0 * fields
    return (-(fields[0] * deriv_x + fields[1] * deriv_y) + DIFFUSION * laplace, deriv_x)

def level_blocks(stacked):
    channels = stacked.shape[0]
    block_depth = math.gcd(NZ, 8)
    return stacked.reshape(channels, NZ // block_depth, block_depth * NCOL).transpose(1, 0, 2)

def unblock(stacked):
    return stacked.transpose(1, 0, 2).reshape(stacked.shape[1], NZ, NCOL)

def closure_forward(features, w_in, w_mid, w_out):
    return unblock(lax.map(lambda blocked: mlp_forward(blocked, w_in, w_mid, w_out), level_blocks(features)))

def closure_backward(features, out_cot, w_in, w_mid, w_out):

    def one_block(totals, pieces):
        feature_cot, grads = mlp_backward(pieces[0], pieces[1], w_in, w_mid, w_out)
        return ((totals[0] + grads[0], totals[1] + grads[1], totals[2] + grads[2]), feature_cot)
    start_grads = (jnp.zeros((HID, 2 * NFIELD), jnp.float32), jnp.zeros((HID, HID), jnp.float32), jnp.zeros((NFIELD, HID), jnp.float32))
    grads, feature_cots = lax.scan(one_block, start_grads, (level_blocks(features), level_blocks(out_cot)))
    return (unblock(feature_cots), grads)

def sediment(rain_water, fall_rate, upward):
    fresh_share = 1.0 / (1.0 + fall_rate)
    retained = fall_rate / (1.0 + fall_rate)

    def settle(carried, level_rain):
        settled = fresh_share * level_rain + retained * carried
        return (settled, settled)
    return lax.scan(settle, jnp.zeros_like(fall_rate), rain_water, reverse=not upward)[1]

def tendency(state, w_in, w_mid, w_out, radiation, fall_rate, live):
    fields = state.reshape(NFIELD, NZ, NX, NY)
    moved, deriv_x = dynamics(fields)
    features = jnp.concatenate([state, deriv_x.reshape(NFIELD, NZ, NCOL)], 0).astype(jnp.bfloat16)
    closure = closure_forward(features, w_in, w_mid, w_out)
    total = moved.reshape(NFIELD, NZ, NCOL) + CLOSURE_GAIN * closure
    heating = jnp.dot(radiation, state[3], precision=lax.Precision.HIGHEST, preferred_element_type=jnp.float32)
    total = total.at[3].add(HEATING_GAIN * heating)
    fallen = sediment(state[5], fall_rate, False)
    return total.at[5].add(FALL_GAIN * live * (fallen - state[5]))

def adjoint_tendency(state, lead, w_in, w_mid, w_out, radiation, fall_rate, live):
    fields = state.reshape(NFIELD, NZ, NX, NY)
    outputs, pullback = jax.vjp(dynamics, fields)
    features = jnp.concatenate([state, outputs[1].reshape(NFIELD, NZ, NCOL)], 0).astype(jnp.bfloat16)
    out_cot = (CLOSURE_GAIN * lead).astype(jnp.bfloat16)
    feature_cot, grads = closure_backward(features, out_cot, w_in, w_mid, w_out)
    field_cot = pullback((lead.reshape(NFIELD, NZ, NX, NY), feature_cot[NFIELD:].reshape(NFIELD, NZ, NX, NY)))[0]
    result = field_cot.reshape(NFIELD, NZ, NCOL) + feature_cot[:NFIELD]
    back_heat = jnp.dot(radiation.T, lead[3], precision=lax.Precision.HIGHEST, preferred_element_type=jnp.float32)
    result = result.at[3].add(HEATING_GAIN * back_heat)
    masked = live * lead[5]
    return (result.at[5].add(FALL_GAIN * (sediment(masked, fall_rate, True) - masked)), grads)

def reference(state, state_cot, w_in, w_mid, w_out, radiation, fall_rate, active):
    live = active.astype(jnp.float32)

    def section_tendency(current):
        return tendency(current, w_in, w_mid, w_out, radiation, fall_rate, live)

    def section_adjoint(current, lead):
        return adjoint_tendency(current, lead, w_in, w_mid, w_out, radiation, fall_rate, live)
    section_one = state + TIME_STEP * section_tendency(state)
    section_two = 0.75 * state + 0.25 * (section_one + TIME_STEP * section_tendency(section_one))
    new_state = state / 3.0 + 2.0 / 3.0 * (section_two + TIME_STEP * section_tendency(section_two))
    lead_two = 2.0 / 3.0 * state_cot
    grad_state = state_cot / 3.0
    back_two, grads_two = section_adjoint(section_two, lead_two)
    cot_two = lead_two + TIME_STEP * back_two
    lead_one = 0.25 * cot_two
    grad_state = grad_state + 0.75 * cot_two
    back_one, grads_one = section_adjoint(section_one, lead_one)
    cot_one = lead_one + TIME_STEP * back_one
    back_zero, grads_zero = section_adjoint(state, cot_one)
    grad_state = grad_state + cot_one + TIME_STEP * back_zero
    grad_in = TIME_STEP * (grads_two[0] + grads_one[0] + grads_zero[0])
    grad_mid = TIME_STEP * (grads_two[1] + grads_one[1] + grads_zero[1])
    grad_out = TIME_STEP * (grads_two[2] + grads_one[2] + grads_zero[2])
    return (new_state, grad_state, grad_in, grad_mid, grad_out)
```

```python
import functools

import jax
import jax.numpy as jnp
from jax import lax
from jax.experimental import pallas as pl
from jax.experimental.pallas import tpu as pltpu
from jax.sharding import PartitionSpec as P

NF = 6
NY = 64
LANES = 128
MESH = pl.DeviceIdType.MESH
F32 = jnp.float32
BF16 = jnp.bfloat16


def mm(a, b, precision=None):
    return lax.dot_general(
        a, b, (((1,), (0,)), ((), ())), precision=precision, preferred_element_type=F32
    )


def mm_t(a, b, precision=None):
    return lax.dot_general(
        a, b, (((1,), (1,)), ((), ())), precision=precision, preferred_element_type=F32
    )


def iota(shape, dim):
    return lax.broadcasted_iota(jnp.int32, shape, dim)


def kernel(
    nz, nx, levels, hid, share,
    state, cot, w_in, w_mid, w_out, rad, fall, act,
    new_state, state_grad, g_mid, g_in, g_out,
    sp, lp, gp, tg, tl, dxs, dys, moved, feats, out_cot, t1s, t2s, h1s, h2s,
    k1, k1t, k2, k2t, wmt, pre1, pre2, by_in, by_out, radt, tab, fcs, acc, a_in, a_out, a_mid,
    pack, part, parts, full,
    halo_send, halo_recv, gz_send, gz_recv, rs_send, rs_recv, ag_send, ag_recv, fin_send, fin_recv,
):
    mz, mx = lax.axis_index("gz"), lax.axis_index("gx")
    left, right = lax.rem(mx + nx - 1, nx), lax.rem(mx + 1, nx)
    rows_all = levels * hid

    barrier = pltpu.get_barrier_semaphore()
    for o in range(1, nz):
        pl.semaphore_signal(
            barrier, inc=1, device_id=(lax.rem(mz + o, nz), mx), device_id_type=MESH
        )
    for o in range(1, nx):
        pl.semaphore_signal(
            barrier, inc=1, device_id=(mz, lax.rem(mx + o, nx)), device_id_type=MESH
        )

    def spread(rows, cols):
        return (iota((rows, cols), 1) // levels == iota((rows, cols), 0)).astype(F32).astype(BF16)

    def spread_t(rows, cols):
        return (iota((rows, cols), 0) // levels == iota((rows, cols), 1)).astype(F32).astype(BF16)

    eye = (iota((hid, hid), 0) == iota((hid, hid), 1)).astype(F32).astype(BF16)
    w1 = mm(w_in[...], spread(2 * NF, 2 * NF * levels))
    w1t = mm_t(spread_t(2 * NF * levels, 2 * NF), w_in[...])
    w2 = mm(spread_t(NF * levels, NF), w_out[...])
    w2t = mm_t(eye, w2.astype(BF16))
    wmt[...] = mm_t(eye, w_mid[...]).astype(BF16)

    def place(z, carry):
        rows = pl.ds(pl.multiple_of(z * hid, hid), hid)
        k1[rows, :] = jnp.where(iota(w1.shape, 1) % levels == z, w1, 0.0).astype(BF16)
        k2t[rows, :] = jnp.where(iota(w2t.shape, 1) % levels == z, w2t, 0.0).astype(BF16)
        k1t[:, rows] = jnp.where(iota(w1t.shape, 0) % levels == z, w1t, 0.0).astype(BF16)
        k2[:, rows] = jnp.where(iota(w2.shape, 0) % levels == z, w2, 0.0).astype(BF16)
        return carry

    lax.fori_loop(0, levels, place, 0)
    radt[...] = rad[...].T

    columns = 2 * LANES
    shape = (levels, columns)
    rate = jnp.broadcast_to(fall[...], shape)
    r1 = rate / (1.0 + rate)
    r2 = r1 * r1
    r4 = r2 * r2
    r8 = r4 * r4
    powers = [r1, r2, r4, r8, r8 * r8]
    up, down = jnp.ones(shape, F32), jnp.ones(shape, F32)
    level = iota(shape, 0)
    for bit in range(5):
        up = jnp.where(((level + 1) // (1 << bit)) % 2 == 1, up * powers[bit], up)
        down = jnp.where(((levels - level) // (1 << bit)) % 2 == 1, down * powers[bit], down)
    for at, value in enumerate(
        powers + [1.0 / (1.0 + rate), jnp.broadcast_to(act[...].astype(F32), shape), down, up]
    ):
        tab[at] = value

    for c in range(2):
        lanes = slice(c * LANES, (c + 1) * LANES)
        sp[0, c + 1] = state[:, :, lanes]
        lp[0, c + 1] = (2.0 / 3.0) * cot[:, :, lanes]
        acc[c] = cot[:, :, lanes] / 3.0
    a_in[...] = jnp.zeros_like(a_in)
    a_out[...] = jnp.zeros_like(a_out)
    a_mid[...] = jnp.zeros_like(a_mid)

    pl.semaphore_wait(barrier, nz - 1 + nx - 1)

    def halo(buf, kind, k):
        return [
            pltpu.make_async_remote_copy(
                src_ref=buf.at[k, 1], dst_ref=buf.at[k, 3],
                send_sem=halo_send.at[kind, k, 0], recv_sem=halo_recv.at[kind, k, 0],
                device_id=(mz, left), device_id_type=MESH,
            ),
            pltpu.make_async_remote_copy(
                src_ref=buf.at[k, 2], dst_ref=buf.at[k, 0],
                send_sem=halo_send.at[kind, k, 1], recv_sem=halo_recv.at[kind, k, 1],
                device_id=(mz, right), device_id_type=MESH,
            ),
        ]

    def level_copies(buf, kind, k):
        sends, receives = [], []
        for o in range(1, nz):
            peer, source = lax.rem(mz + o, nz), lax.rem(mz + nz - o, nz)
            sends.append(
                pltpu.make_async_remote_copy(
                    src_ref=buf.at[k, mz], dst_ref=buf.at[k, mz],
                    send_sem=gz_send.at[kind, k, o], recv_sem=gz_recv.at[kind, k, mz],
                    device_id=(peer, mx), device_id_type=MESH,
                )
            )
            receives.append(
                pltpu.make_async_remote_copy(
                    src_ref=buf.at[k, mz], dst_ref=buf.at[k, source],
                    send_sem=gz_send.at[kind, k, o], recv_sem=gz_recv.at[kind, k, source],
                    device_id=(peer, mx), device_id_type=MESH,
                )
            )
        return sends, receives

    lane = iota((1, levels, LANES), 2)
    low = lane < NY
    y_last, y_first = lane % NY == NY - 1, lane % NY == 0
    depth = iota((levels, LANES), 0)

    def along_x(chunks):
        turned = [pltpu.roll(chunk, NY, 2) for chunk in chunks]
        out = []
        for i in (1, 2):
            plus = jnp.where(low, turned[i], turned[i + 1])
            minus = jnp.where(low, turned[i - 1], turned[i])
            out.append((plus, minus, (8.0 * (plus - minus) - (chunks[i + 1] - chunks[i - 1])) / 12.0))
        return out

    def along_y(chunk):
        plus = jnp.where(y_last, pltpu.roll(chunk, NY - 1, 2), pltpu.roll(chunk, LANES - 1, 2))
        minus = jnp.where(y_first, pltpu.roll(chunk, NY + 1, 2), pltpu.roll(chunk, 1, 2))
        return plus, minus

    def settle(source, lanes, downward):
        value = tab[5, :, lanes] * source
        for bit in range(4):
            step = 1 << bit
            if downward:
                moved_by = pltpu.roll(value, levels - step, 0)
                inside = depth < levels - step
            else:
                moved_by = pltpu.roll(value, step, 0)
                inside = depth >= step
            value = value + tab[bit, :, lanes] * jnp.where(inside, moved_by, 0.0)
        return value

    def inflow(buf, k, lanes, downward):
        total = jnp.zeros((8, LANES), F32)
        order = range(nz - 1, 0, -1) if downward else range(nz - 1)
        for j in order:
            reached = j > mz if downward else j < mz
            following = buf[k, j, levels:, lanes] + tab[4, 0:8, lanes] * total
            total = jnp.where(reached, following, total)
        return total[0:1]

    def chunk_lanes(c):
        return slice(c * LANES, (c + 1) * LANES)

    def forward(k, carry):
        own = [sp[k, 1], sp[k, 2]]
        halos = halo(sp, 0, k)
        for copy in halos:
            copy.start()
        local = []
        for c in range(2):
            value = settle(own[c][5], chunk_lanes(c), True)
            local.append(value)
            tg[k, mz, 0:levels, chunk_lanes(c)] = own[c][3]
            tg[k, mz, levels:, chunk_lanes(c)] = jnp.broadcast_to(value[0:1], (8, LANES))
        sends, receives = level_copies(tg, 0, k)
        for copy in sends:
            copy.start()
        for copy in halos:
            copy.wait_recv()
        x_sides = along_x([sp[k, 0], own[0], own[1], sp[k, 3]])
        for c in range(2):
            y_plus, y_minus = along_y(own[c])
            x_plus, x_minus, deriv_x = x_sides[c]
            deriv_y = (y_plus - y_minus) / 2.0
            laplace = x_plus + x_minus + y_plus + y_minus - 4.0 * own[c]
            dxs[k, c] = deriv_x
            dys[k, c] = deriv_y
            moved[c] = -(own[c][0:1] * deriv_x + own[c][1:2] * deriv_y) + 0.1 * laplace
            feats[k, 0 : NF * levels, chunk_lanes(c)] = (
                own[c].reshape(NF * levels, LANES).astype(BF16)
            )
            feats[k, NF * levels :, chunk_lanes(c)] = (
                deriv_x.reshape(NF * levels, LANES).astype(BF16)
            )

        def layers(group, inner):
            for j in range(4):
                rows = pl.ds(pl.multiple_of((group * 4 + j) * hid, hid), hid)
                t1 = jnp.tanh(mm(k1[rows, :], feats[k]))
                t1s[k, rows, :] = t1
                h1 = t1.astype(BF16)
                h1s[k, rows, :] = h1
                t2 = jnp.tanh(mm(w_mid[...], h1))
                t2s[k, rows, :] = t2
                h2s[k, rows, :] = t2.astype(BF16)
            return inner

        lax.fori_loop(0, levels // 4, layers, 0)
        closure = mm(k2[...], h2s[k])
        for copy in receives:
            copy.wait_recv()
        heat = mm(
            rad[pl.ds(pl.multiple_of(mz * levels, levels), levels), :],
            tg[k, :, 0:levels, :].reshape(nz * levels, columns),
            lax.Precision.HIGHEST,
        )
        keep = jnp.where(k == 0, 0.0, jnp.where(k == 1, 0.75, 1.0 / 3.0))
        take = jnp.where(k == 0, 1.0, jnp.where(k == 1, 0.25, 2.0 / 3.0))
        for c in range(2):
            lanes = chunk_lanes(c)
            total = moved[c] + closure[:, lanes].reshape(NF, levels, LANES)
            fallen = local[c] + tab[7, :, lanes] * inflow(tg, k, lanes, True)
            total = jnp.concatenate(
                [
                    total[0:3],
                    total[3:4] + heat[:, lanes][None],
                    total[4:5],
                    total[5:6] + (tab[6, :, lanes] * (fallen - own[c][5]))[None],
                ],
                0,
            )
            sp[k + 1, c + 1] = keep * state[:, :, lanes] + take * (own[c] + 0.25 * total)
        for copy in halos + sends:
            copy.wait_send()
        return carry

    lax.fori_loop(0, 3, forward, 0)
    for c in range(2):
        new_state[:, :, chunk_lanes(c)] = sp[3, c + 1]


    def gathered(cols):
        at = iota((levels * 16, cols), 0)
        return ((at % 16) * levels + at // 16 == iota((levels * 16, cols), 1)).astype(F32).astype(BF16)

    def backward(i, carry):
        k = 2 - i
        lam = [lp[i, 1], lp[i, 2]]
        halos = halo(lp, 1, i)
        for copy in halos:
            copy.start()
        local, masked = [], []
        for c in range(2):
            lanes = chunk_lanes(c)
            source = tab[6, :, lanes] * lam[c][5]
            value = settle(source, lanes, False)
            masked.append(source)
            local.append(value)
            tl[i, mz, 0:levels, lanes] = lam[c][3]
            tl[i, mz, levels:, lanes] = jnp.broadcast_to(value[levels - 1 : levels], (8, LANES))
            out_cot[:, lanes] = lam[c].reshape(NF * levels, LANES).astype(BF16)
        sends, receives = level_copies(tl, 1, i)
        for copy in sends:
            copy.start()

        def layers(group, inner):
            for j in range(4):
                rows = pl.ds(pl.multiple_of((group * 4 + j) * hid, hid), hid)
                t2 = t2s[k, rows, :]
                p2 = (mm(k2t[rows, :], out_cot[...]) * (1.0 - t2 * t2)).astype(BF16)
                pre2[rows, :] = p2
                t1 = t1s[k, rows, :]
                pre1[rows, :] = (mm(wmt[...], p2) * (1.0 - t1 * t1)).astype(BF16)
            return inner

        lax.fori_loop(0, levels // 4, layers, 0)
        feature_cot = mm(k1t[...], pre1[...])
        for c in range(2):
            lanes = chunk_lanes(c)
            fcs[c] = feature_cot[0 : NF * levels, lanes].reshape(NF, levels, LANES)
            gp[i, c + 1] = (
                feature_cot[NF * levels :, lanes].reshape(NF, levels, LANES)
                - sp[k, c + 1, 0:1] * lp[i, c + 1]
            )
        rims = halo(gp, 2, i)
        for copy in rims:
            copy.start()

        by_in[...] = mm(gathered(2 * NF * levels), feats[k]).astype(BF16)
        by_out[...] = mm(gathered(NF * levels), out_cot[...]).astype(BF16)

        def terms(group, inner):
            s_in, s_out, s_mid = inner
            for j in range(4):
                z = group * 4 + j
                rows = pl.ds(pl.multiple_of(z * hid, hid), hid)
                few = pl.ds(pl.multiple_of(z * 16, 16), 16)
                s_mid = s_mid + mm_t(pre2[rows, :], h1s[k, rows, :])
                s_in = s_in + mm_t(by_in[few, :], pre1[rows, :])
                s_out = s_out + mm_t(by_out[few, :], h2s[k, rows, :])
            return s_in, s_out, s_mid

        s_in, s_out, s_mid = lax.fori_loop(
            0, levels // 4, terms, (a_in[...], a_out[...], a_mid[...])
        )
        a_in[...] = s_in
        a_out[...] = s_out
        a_mid[...] = s_mid

        for copy in halos:
            copy.wait_recv()
        for copy in receives:
            copy.wait_recv()
        heat = mm(
            radt[pl.ds(pl.multiple_of(mz * levels, levels), levels), :],
            tl[i, :, 0:levels, :].reshape(nz * levels, columns),
            lax.Precision.HIGHEST,
        )
        lam_sides = along_x([lp[i, 0], lam[0], lam[1], lp[i, 3]])
        for copy in rims:
            copy.wait_recv()
        g_sides = along_x([gp[i, 0], gp[i, 1], gp[i, 2], gp[i, 3]])
        weight = jnp.where(k == 0, 1.0, jnp.where(k == 1, 0.0, 0.75))
        share_on = jnp.where(k == 2, 0.25, 1.0)
        for c in range(2):
            lanes = chunk_lanes(c)
            now = lam[c]
            y_plus, y_minus = along_y(now)
            x_plus, x_minus, _ = lam_sides[c]
            carried_plus, carried_minus = along_y(sp[k, c + 1, 1:2] * now)
            back = (
                (carried_plus - carried_minus) / 2.0
                - g_sides[c][2]
                + 0.1 * (x_plus + x_minus + y_plus + y_minus - 4.0 * now)
                + fcs[c]
            )
            pulled = local[c] + tab[8, :, lanes] * inflow(tl, i, lanes, False)
            back = jnp.concatenate(
                [
                    back[0:1] - jnp.sum(now * dxs[k, c], axis=0, keepdims=True),
                    back[1:2] - jnp.sum(now * dys[k, c], axis=0, keepdims=True),
                    back[2:3],
                    back[3:4] + heat[:, lanes][None],
                    back[4:5],
                    back[5:6] + (pulled - masked[c])[None],
                ],
                0,
            )
            whole = now + 0.25 * back
            acc[c] = acc[c] + weight * whole
            lp[i + 1, c + 1] = share_on * whole
        for copy in halos + sends + rims:
            copy.wait_send()
        return carry

    lax.fori_loop(0, 3, backward, 0)
    for c in range(2):
        state_grad[:, :, chunk_lanes(c)] = acc[c]

    total_rows = nz * share
    everything = jnp.concatenate(
        [
            a_mid[...],
            a_in[...],
            a_out[0:8, :],
            jnp.zeros((total_rows - hid - 24, LANES), F32),
        ],
        0,
    )
    pack[...] = everything.reshape(nz, share, LANES)
    scatter = []
    for o in range(1, nz):
        peer = lax.rem(mz + o, nz)
        scatter.append(
            pltpu.make_async_remote_copy(
                src_ref=pack.at[peer], dst_ref=part.at[o],
                send_sem=rs_send.at[o], recv_sem=rs_recv.at[o],
                device_id=(peer, mx), device_id_type=MESH,
            )
        )
    for copy in scatter:
        copy.start()
    mine = pack[mz]
    for o in range(1, nz):
        scatter[o - 1].wait_recv()
        mine = mine + part[o]
    parts[mx] = mine

    sends, receives = [], []
    for o in range(1, nx):
        peer, source = lax.rem(mx + o, nx), lax.rem(mx + nx - o, nx)
        for dst, to in ((mx, sends), (source, receives)):
            to.append(
                pltpu.make_async_remote_copy(
                    src_ref=parts.at[mx], dst_ref=parts.at[dst],
                    send_sem=ag_send.at[o], recv_sem=ag_recv.at[dst],
                    device_id=(mz, peer), device_id_type=MESH,
                )
            )
    for copy in sends:
        copy.start()
    for copy in receives:
        copy.wait_recv()
    summed = parts[0]
    for j in range(1, nx):
        summed = summed + parts[j]
    full[mz] = 0.25 * summed

    sends_z, receives_z = [], []
    for o in range(1, nz):
        peer, source = lax.rem(mz + o, nz), lax.rem(mz + nz - o, nz)
        for dst, to in ((mz, sends_z), (source, receives_z)):
            to.append(
                pltpu.make_async_remote_copy(
                    src_ref=full.at[mz], dst_ref=full.at[dst],
                    send_sem=fin_send.at[o], recv_sem=fin_recv.at[dst],
                    device_id=(peer, mx), device_id_type=MESH,
                )
            )
    for copy in sends_z:
        copy.start()
    for copy in receives_z:
        copy.wait_recv()
    result = full[...].reshape(total_rows, LANES)
    g_mid[...] = result[0:hid]
    g_in[...] = result[hid : hid + 16]
    g_out[...] = result[hid + 16 : hid + 24]
    for copy in scatter + sends + sends_z:
        copy.wait_send()


def on_device(nz, nx, state, state_cot, w_in, w_mid, w_out, radiation, fall_rate, active):
    fields, levels, columns = state.shape
    hid = w_in.shape[0]
    assert fields == NF and columns == 2 * LANES and hid == LANES and levels == 16
    share = -(-(hid + 24) // (8 * nz)) * 8
    cells = levels * hid
    wide = NF * levels
    chunk = (4, NF, levels, LANES)
    two = (2, NF, levels, LANES)
    dma = pltpu.SemaphoreType.DMA
    vmem = pltpu.VMEM
    scratch = [
        vmem((4,) + chunk, F32),
        vmem((4,) + chunk, F32),
        vmem((3,) + chunk, F32),
        vmem((3, nz, levels + 8, columns), F32),
        vmem((3, nz, levels + 8, columns), F32),
        vmem((3,) + two, F32),
        vmem((3,) + two, F32),
        vmem(two, F32),
        vmem((3, 2 * wide, columns), BF16),
        vmem((wide, columns), BF16),
        vmem((3, cells, columns), F32),
        vmem((3, cells, columns), F32),
        vmem((3, cells, columns), BF16),
        vmem((3, cells, columns), BF16),
        vmem((cells, 2 * wide), BF16),
        vmem((2 * wide, cells), BF16),
        vmem((wide, cells), BF16),
        vmem((cells, wide), BF16),
        vmem((hid, hid), BF16),
        vmem((cells, columns), BF16),
        vmem((cells, columns), BF16),
        vmem((levels * 16, columns), BF16),
        vmem((levels * 16, columns), BF16),
        vmem(radiation.shape, F32),
        vmem((9, levels, columns), F32),
        vmem(two, F32),
        vmem(two, F32),
        vmem((16, hid), F32),
        vmem((16, hid), F32),
        vmem((hid, hid), F32),
        vmem((nz, share, LANES), F32),
        vmem((nz, share, LANES), F32),
        vmem((nx, share, LANES), F32),
        vmem((nz, share, LANES), F32),
        dma((3, 3, 2)), dma((3, 3, 2)),
        dma((2, 3, nz)), dma((2, 3, nz)),
        dma((nz,)), dma((nz,)),
        dma((nx,)), dma((nx,)),
        dma((nz,)), dma((nz,)),
    ]
    whole = pl.BlockSpec(memory_space=pltpu.VMEM)
    new_state, state_grad, g_mid, g_in, g_out = pl.pallas_call(
        functools.partial(kernel, nz, nx, levels, hid, share),
        out_shape=(
            jax.ShapeDtypeStruct(state.shape, F32),
            jax.ShapeDtypeStruct(state.shape, F32),
            jax.ShapeDtypeStruct((hid, hid), F32),
            jax.ShapeDtypeStruct((16, hid), F32),
            jax.ShapeDtypeStruct((8, hid), F32),
        ),
        in_specs=[whole] * 8,
        out_specs=[whole] * 5,
        scratch_shapes=scratch,
        compiler_params=pltpu.CompilerParams(
            collective_id=0, has_side_effects=True, vmem_limit_bytes=48 * 1024 * 1024
        ),
        name="adjoint_step",
    )(
        state, state_cot, w_in, w_mid, w_out, radiation,
        fall_rate.reshape(1, columns), active.reshape(1, columns),
    )
    return new_state, state_grad, g_in[: 2 * NF].T, g_mid, g_out[:NF]


def solution(mesh):
    placed = (P(None, "gz", "gx"), P(None, "gz", "gx"), P(), P(), P(), P(), P("gx"), P("gx"))
    return jax.shard_map(
        functools.partial(on_device, mesh.shape["gz"], mesh.shape["gx"]),
        mesh=mesh,
        in_specs=placed,
        out_specs=(P(None, "gz", "gx"), P(None, "gz", "gx"), P(), P(), P()),
        check_vma=False,
    )
```

```python
import functools

import jax
import jax.numpy as jnp
from jax import lax
from jax.experimental import pallas as pl
from jax.experimental.pallas import tpu as pltpu
from jax.sharding import PartitionSpec as P

NF = 6
NY = 64
LANES = 128
LEVEL_BITS = 4
MESH = pl.DeviceIdType.MESH
F32 = jnp.float32
BF16 = jnp.bfloat16


def mm(a, b, precision=None):
    return lax.dot_general(
        a, b, (((1,), (0,)), ((), ())), precision=precision, preferred_element_type=F32
    )


def mm_t(a, b, precision=None):
    return lax.dot_general(
        a, b, (((1,), (1,)), ((), ())), precision=precision, preferred_element_type=F32
    )


def iota(shape, dim):
    return lax.broadcasted_iota(jnp.int32, shape, dim)


def kernel(
    nz, nx, levels, hid, share,
    state_hbm, cot_hbm, w_in_hbm, w_mid_hbm, w_out_hbm, rad_hbm, fall_hbm, act_hbm,
    new_state, state_grad, g_mid, g_in, g_out,
    state, cot, w_in, w_mid, w_out, rad, fall, act, pick_in, pick_out,
    sp, lp, gp, tg, tl, dxs, dys, moved, feats, out_cot, t1s, t2s, h1s, h2s,
    k1, k1t, k2, k2t, wmt, pre1, pre2, by_in, by_out, radt, tab, fcs, acc, a_in, a_out, a_mid,
    pack, part, parts, full,
    load_sem, store_sem, halo_send, halo_recv, gz_send, gz_recv, rs_send, rs_recv, ag_send, ag_recv, fin_send, fin_recv,
):
    mz, mx = lax.axis_index("gz"), lax.axis_index("gx")
    left, right = lax.rem(mx + nx - 1, nx), lax.rem(mx + 1, nx)
    rows_all = levels * hid

    barrier = pltpu.get_barrier_semaphore()
    for o in range(1, nz):
        pl.semaphore_signal(
            barrier, inc=1, device_id=(lax.rem(mz + o, nz), mx), device_id_type=MESH
        )
    for o in range(1, nx):
        pl.semaphore_signal(
            barrier, inc=1, device_id=(mz, lax.rem(mx + o, nx)), device_id_type=MESH
        )

    loads = [
        pltpu.make_async_copy(src, dst, load_sem.at[at])
        for at, (src, dst) in enumerate(
            [
                (state_hbm, state), (cot_hbm, cot), (w_in_hbm, w_in), (w_mid_hbm, w_mid),
                (w_out_hbm, w_out), (rad_hbm, rad), (fall_hbm, fall), (act_hbm, act),
            ]
        )
    ]
    for copy in loads:
        copy.start()
    a_in[...] = jnp.zeros_like(a_in)
    a_out[...] = jnp.zeros_like(a_out)
    a_mid[...] = jnp.zeros_like(a_mid)
    for copy in loads:
        copy.wait()

    def spread_t(rows, cols):
        return (iota((rows, cols), 0) >> LEVEL_BITS == iota((rows, cols), 1)).astype(F32).astype(BF16)

    eye = (iota((hid, hid), 0) == iota((hid, hid), 1)).astype(F32).astype(BF16)
    w1t = mm(spread_t(2 * NF * levels, 2 * NF), w_in[...])
    w1 = mm_t(eye, w1t.astype(BF16))
    w2 = mm(spread_t(NF * levels, NF), w_out[...])
    w2t = mm_t(eye, w2.astype(BF16))
    wmt[...] = mm_t(eye, w_mid[...]).astype(BF16)

    def place(z, carry):
        rows = pl.ds(pl.multiple_of(z * hid, hid), hid)
        k1[rows, :] = jnp.where(iota(w1.shape, 1) & (levels - 1) == z, w1, 0.0).astype(BF16)
        k2t[rows, :] = jnp.where(iota(w2t.shape, 1) & (levels - 1) == z, w2t, 0.0).astype(BF16)
        k1t[:, rows] = jnp.where(iota(w1t.shape, 0) & (levels - 1) == z, w1t, 0.0).astype(BF16)
        k2[:, rows] = jnp.where(iota(w2.shape, 0) & (levels - 1) == z, w2, 0.0).astype(BF16)
        return carry

    lax.fori_loop(0, levels, place, 0)
    radt[...] = rad[...].T

    def gathered(cols):
        at = iota((levels * 16, cols), 0)
        return ((at & 15) * levels + (at >> 4) == iota((levels * 16, cols), 1)).astype(F32).astype(BF16)

    pick_in[...] = gathered(2 * NF * levels)
    pick_out[...] = gathered(NF * levels)

    columns = 2 * LANES
    shape = (levels, columns)
    rate = jnp.broadcast_to(fall[...], shape)
    r1 = rate / (1.0 + rate)
    r2 = r1 * r1
    r4 = r2 * r2
    r8 = r4 * r4
    powers = [r1, r2, r4, r8, r8 * r8]
    up, down = jnp.ones(shape, F32), jnp.ones(shape, F32)
    level = iota(shape, 0)
    for bit in range(5):
        up = jnp.where(((level + 1) >> bit) & 1 == 1, up * powers[bit], up)
        down = jnp.where(((levels - level) >> bit) & 1 == 1, down * powers[bit], down)
    for at, value in enumerate(
        powers + [1.0 / (1.0 + rate), jnp.broadcast_to(act[...].astype(F32), shape), down, up]
    ):
        tab[at] = value

    for c in range(2):
        lanes = slice(c * LANES, (c + 1) * LANES)
        sp[0, c + 1] = state[:, :, lanes]
        lp[0, c + 1] = (2.0 / 3.0) * cot[:, :, lanes]
        acc[c] = cot[:, :, lanes] / 3.0
    pl.semaphore_wait(barrier, nz - 1 + nx - 1)

    def halo(buf, kind, k):
        return [
            pltpu.make_async_remote_copy(
                src_ref=buf.at[k, 1], dst_ref=buf.at[k, 3],
                send_sem=halo_send.at[kind, k, 0], recv_sem=halo_recv.at[kind, k, 0],
                device_id=(mz, left), device_id_type=MESH,
            ),
            pltpu.make_async_remote_copy(
                src_ref=buf.at[k, 2], dst_ref=buf.at[k, 0],
                send_sem=halo_send.at[kind, k, 1], recv_sem=halo_recv.at[kind, k, 1],
                device_id=(mz, right), device_id_type=MESH,
            ),
        ]

    def level_copies(buf, kind, k):
        sends, receives = [], []
        for o in range(1, nz):
            peer, source = lax.rem(mz + o, nz), lax.rem(mz + nz - o, nz)
            sends.append(
                pltpu.make_async_remote_copy(
                    src_ref=buf.at[k, mz], dst_ref=buf.at[k, mz],
                    send_sem=gz_send.at[kind, k, o], recv_sem=gz_recv.at[kind, k, mz],
                    device_id=(peer, mx), device_id_type=MESH,
                )
            )
            receives.append(
                pltpu.make_async_remote_copy(
                    src_ref=buf.at[k, mz], dst_ref=buf.at[k, source],
                    send_sem=gz_send.at[kind, k, o], recv_sem=gz_recv.at[kind, k, source],
                    device_id=(peer, mx), device_id_type=MESH,
                )
            )
        return sends, receives

    lane = iota((1, levels, LANES), 2)
    low = lane < NY
    y_last, y_first = lane & (NY - 1) == NY - 1, lane & (NY - 1) == 0
    depth = iota((levels, LANES), 0)

    def along_x(chunks):
        turned = [pltpu.roll(chunk, NY, 2) for chunk in chunks]
        out = []
        for i in (1, 2):
            plus = jnp.where(low, turned[i], turned[i + 1])
            minus = jnp.where(low, turned[i - 1], turned[i])
            out.append((plus, minus, (8.0 * (plus - minus) - (chunks[i + 1] - chunks[i - 1])) * (1.0 / 12.0)))
        return out

    def along_y(chunk):
        plus = jnp.where(y_last, pltpu.roll(chunk, NY - 1, 2), pltpu.roll(chunk, LANES - 1, 2))
        minus = jnp.where(y_first, pltpu.roll(chunk, NY + 1, 2), pltpu.roll(chunk, 1, 2))
        return plus, minus

    def settle(source, lanes, downward):
        value = tab[5, :, lanes] * source
        for bit in range(4):
            step = 1 << bit
            if downward:
                moved_by = pltpu.roll(value, levels - step, 0)
                inside = depth < levels - step
            else:
                moved_by = pltpu.roll(value, step, 0)
                inside = depth >= step
            value = value + tab[bit, :, lanes] * jnp.where(inside, moved_by, 0.0)
        return value

    def inflow(buf, k, lanes, downward):
        total = jnp.zeros((8, LANES), F32)
        order = range(nz - 1, 0, -1) if downward else range(nz - 1)
        for j in order:
            reached = j > mz if downward else j < mz
            following = buf[k, j, levels:, lanes] + tab[4, 0:8, lanes] * total
            total = jnp.where(reached, following, total)
        return total[0:1]

    def chunk_lanes(c):
        return slice(c * LANES, (c + 1) * LANES)

    def forward(k, carry):
        own = [sp[k, 1], sp[k, 2]]
        halos = halo(sp, 0, k)
        for copy in halos:
            copy.start()
        local = []
        for c in range(2):
            value = settle(own[c][5], chunk_lanes(c), True)
            local.append(value)
            tg[k, mz, 0:levels, chunk_lanes(c)] = own[c][3]
            tg[k, mz, levels:, chunk_lanes(c)] = jnp.broadcast_to(value[0:1], (8, LANES))
        sends, receives = level_copies(tg, 0, k)
        for copy in sends:
            copy.start()
        for copy in halos:
            copy.wait_recv()
        x_sides = along_x([sp[k, 0], own[0], own[1], sp[k, 3]])
        for c in range(2):
            y_plus, y_minus = along_y(own[c])
            x_plus, x_minus, deriv_x = x_sides[c]
            deriv_y = (y_plus - y_minus) * 0.5
            laplace = x_plus + x_minus + y_plus + y_minus - 4.0 * own[c]
            dxs[k, c] = deriv_x
            dys[k, c] = deriv_y
            moved[c] = -(own[c][0:1] * deriv_x + own[c][1:2] * deriv_y) + 0.1 * laplace
            feats[k, 0 : NF * levels, chunk_lanes(c)] = (
                own[c].reshape(NF * levels, LANES).astype(BF16)
            )
            feats[k, NF * levels :, chunk_lanes(c)] = (
                deriv_x.reshape(NF * levels, LANES).astype(BF16)
            )

        def layers(group, inner):
            block = pl.ds(pl.multiple_of(group * (4 * hid), 4 * hid), 4 * hid)
            t1 = jnp.tanh(mm(k1[block, :], feats[k]))
            t1s[k, block, :] = t1
            h1 = t1.astype(BF16)
            h1s[k, block, :] = h1
            for j in range(4):
                rows = pl.ds(pl.multiple_of((group * 4 + j) * hid, hid), hid)
                t2 = jnp.tanh(mm(w_mid[...], h1[j * hid : (j + 1) * hid]))
                t2s[k, rows, :] = t2
                h2s[k, rows, :] = t2.astype(BF16)
            return inner

        lax.fori_loop(0, levels // 4, layers, 0)
        closure = mm(k2[...], h2s[k])
        for copy in receives:
            copy.wait_recv()
        heat = mm(
            rad[pl.ds(pl.multiple_of(mz * levels, levels), levels), :],
            tg[k, :, 0:levels, :].reshape(nz * levels, columns),
            lax.Precision.HIGHEST,
        )
        keep = jnp.where(k == 0, 0.0, jnp.where(k == 1, 0.75, 1.0 / 3.0))
        take = jnp.where(k == 0, 1.0, jnp.where(k == 1, 0.25, 2.0 / 3.0))
        for c in range(2):
            lanes = chunk_lanes(c)
            total = moved[c] + closure[:, lanes].reshape(NF, levels, LANES)
            fallen = local[c] + tab[7, :, lanes] * inflow(tg, k, lanes, True)
            total = jnp.concatenate(
                [
                    total[0:3],
                    total[3:4] + heat[:, lanes][None],
                    total[4:5],
                    total[5:6] + (tab[6, :, lanes] * (fallen - own[c][5]))[None],
                ],
                0,
            )
            sp[k + 1, c + 1] = keep * state[:, :, lanes] + take * (own[c] + 0.25 * total)
        for copy in halos + sends:
            copy.wait_send()
        return carry

    lax.fori_loop(0, 3, forward, 0)
    stores = []
    for c in range(2):
        stores.append(
            pltpu.make_async_copy(
                sp.at[3, c + 1], new_state.at[:, :, chunk_lanes(c)], store_sem.at[c]
            )
        )
        stores[-1].start()


    total_rows = nz * share
    scatter = []
    for o in range(1, nz):
        peer = lax.rem(mz + o, nz)
        scatter.append(
            pltpu.make_async_remote_copy(
                src_ref=pack.at[peer], dst_ref=part.at[o],
                send_sem=rs_send.at[o], recv_sem=rs_recv.at[o],
                device_id=(peer, mx), device_id_type=MESH,
            )
        )

    def backward(i, carry):
        k = 2 - i
        lam = [lp[i, 1], lp[i, 2]]
        halos = halo(lp, 1, i)
        for copy in halos:
            copy.start()
        local, masked = [], []
        for c in range(2):
            lanes = chunk_lanes(c)
            source = tab[6, :, lanes] * lam[c][5]
            value = settle(source, lanes, False)
            masked.append(source)
            local.append(value)
            tl[i, mz, 0:levels, lanes] = lam[c][3]
            tl[i, mz, levels:, lanes] = jnp.broadcast_to(value[levels - 1 : levels], (8, LANES))
            out_cot[:, lanes] = lam[c].reshape(NF * levels, LANES).astype(BF16)
        sends, receives = level_copies(tl, 1, i)
        for copy in sends:
            copy.start()

        def layers(group, inner):
            block = pl.ds(pl.multiple_of(group * (4 * hid), 4 * hid), 4 * hid)
            t2 = t2s[k, block, :]
            p2 = (mm(k2t[block, :], out_cot[...]) * (1.0 - t2 * t2)).astype(BF16)
            pre2[block, :] = p2
            for j in range(4):
                rows = pl.ds(pl.multiple_of((group * 4 + j) * hid, hid), hid)
                t1 = t1s[k, rows, :]
                back = mm(wmt[...], p2[j * hid : (j + 1) * hid])
                pre1[rows, :] = (back * (1.0 - t1 * t1)).astype(BF16)
            return inner

        lax.fori_loop(0, levels // 4, layers, 0)
        feature_cot = mm(k1t[...], pre1[...])
        for c in range(2):
            lanes = chunk_lanes(c)
            fcs[c] = feature_cot[0 : NF * levels, lanes].reshape(NF, levels, LANES)
            gp[i, c + 1] = (
                feature_cot[NF * levels :, lanes].reshape(NF, levels, LANES)
                - sp[k, c + 1, 0:1] * lp[i, c + 1]
            )
        rims = halo(gp, 2, i)
        for copy in rims:
            copy.start()

        by_in[...] = mm(pick_in[...], feats[k]).astype(BF16)
        by_out[...] = mm(pick_out[...], out_cot[...]).astype(BF16)

        def terms(group, inner):
            s_in, s_out, s_mid = inner
            for j in range(4):
                z = group * 4 + j
                rows = pl.ds(pl.multiple_of(z * hid, hid), hid)
                few = pl.ds(pl.multiple_of(z * 16, 16), 16)
                s_mid = s_mid + mm_t(pre2[rows, :], h1s[k, rows, :])
                s_in = s_in + mm_t(by_in[few, :], pre1[rows, :])
                s_out = s_out + mm_t(by_out[few, :], h2s[k, rows, :])
            return s_in, s_out, s_mid

        s_in, s_out, s_mid = lax.fori_loop(
            0, levels // 4, terms, (a_in[...], a_out[...], a_mid[...])
        )
        a_in[...] = s_in
        a_out[...] = s_out
        a_mid[...] = s_mid

        @pl.when(k == 0)
        def _():
            everything = jnp.concatenate(
                [
                    a_mid[...],
                    a_in[...],
                    a_out[0:8, :],
                    jnp.zeros((total_rows - hid - 24, LANES), F32),
                ],
                0,
            )
            pack[...] = everything.reshape(nz, share, LANES)
            for copy in scatter:
                copy.start()

        for copy in halos:
            copy.wait_recv()
        for copy in receives:
            copy.wait_recv()
        heat = mm(
            radt[pl.ds(pl.multiple_of(mz * levels, levels), levels), :],
            tl[i, :, 0:levels, :].reshape(nz * levels, columns),
            lax.Precision.HIGHEST,
        )
        lam_sides = along_x([lp[i, 0], lam[0], lam[1], lp[i, 3]])
        for copy in rims:
            copy.wait_recv()
        g_sides = along_x([gp[i, 0], gp[i, 1], gp[i, 2], gp[i, 3]])
        weight = jnp.where(k == 0, 1.0, jnp.where(k == 1, 0.0, 0.75))
        share_on = jnp.where(k == 2, 0.25, 1.0)
        for c in range(2):
            lanes = chunk_lanes(c)
            now = lam[c]
            y_plus, y_minus = along_y(now)
            x_plus, x_minus, _ = lam_sides[c]
            carried_plus, carried_minus = along_y(sp[k, c + 1, 1:2] * now)
            back = (
                (carried_plus - carried_minus) * 0.5
                - g_sides[c][2]
                + 0.1 * (x_plus + x_minus + y_plus + y_minus - 4.0 * now)
                + fcs[c]
            )
            pulled = local[c] + tab[8, :, lanes] * inflow(tl, i, lanes, False)
            back = jnp.concatenate(
                [
                    back[0:1] - jnp.sum(now * dxs[k, c], axis=0, keepdims=True),
                    back[1:2] - jnp.sum(now * dys[k, c], axis=0, keepdims=True),
                    back[2:3],
                    back[3:4] + heat[:, lanes][None],
                    back[4:5],
                    back[5:6] + (pulled - masked[c])[None],
                ],
                0,
            )
            whole = now + 0.25 * back
            acc[c] = acc[c] + weight * whole
            lp[i + 1, c + 1] = share_on * whole
        for copy in halos + sends + rims:
            copy.wait_send()
        return carry

    lax.fori_loop(0, 3, backward, 0)
    for c in range(2):
        stores.append(
            pltpu.make_async_copy(
                acc.at[c], state_grad.at[:, :, chunk_lanes(c)], store_sem.at[2 + c]
            )
        )
        stores[-1].start()

    mine = pack[mz]
    for o in range(1, nz):
        scatter[o - 1].wait_recv()
        mine = mine + part[o]
    parts[mx] = mine

    sends, receives = [], []
    for o in range(1, nx):
        peer, source = lax.rem(mx + o, nx), lax.rem(mx + nx - o, nx)
        for dst, to in ((mx, sends), (source, receives)):
            to.append(
                pltpu.make_async_remote_copy(
                    src_ref=parts.at[mx], dst_ref=parts.at[dst],
                    send_sem=ag_send.at[o], recv_sem=ag_recv.at[dst],
                    device_id=(mz, peer), device_id_type=MESH,
                )
            )
    for copy in sends:
        copy.start()
    for copy in receives:
        copy.wait_recv()
    summed = parts[0]
    for j in range(1, nx):
        summed = summed + parts[j]

    def quarter(index):
        return pl.ds(pl.multiple_of(index * share, 8), share)

    full[quarter(mz), :] = 0.25 * summed

    sends_z, receives_z = [], []
    for o in range(1, nz):
        peer, source = lax.rem(mz + o, nz), lax.rem(mz + nz - o, nz)
        for dst, to in ((mz, sends_z), (source, receives_z)):
            to.append(
                pltpu.make_async_remote_copy(
                    src_ref=full.at[quarter(mz)], dst_ref=full.at[quarter(dst)],
                    send_sem=fin_send.at[o], recv_sem=fin_recv.at[dst],
                    device_id=(peer, mx), device_id_type=MESH,
                )
            )
    for copy in sends_z:
        copy.start()
    for copy in receives_z:
        copy.wait_recv()
    for at, (out, first, count) in enumerate(
        ((g_mid, 0, hid), (g_in, hid, 2 * NF), (g_out, hid + 16, NF))
    ):
        stores.append(
            pltpu.make_async_copy(full.at[first : first + count], out, store_sem.at[4 + at])
        )
        stores[-1].start()
    for copy in stores:
        copy.wait()
    for copy in scatter + sends + sends_z:
        copy.wait_send()


def write_out(*refs):
    copies = [
        pltpu.make_async_copy(refs[at], refs[5 + at], refs[10].at[at]) for at in range(5)
    ]
    for copy in copies:
        copy.start()
    for copy in copies:
        copy.wait()


def on_device(nz, nx, state, state_cot, w_in, w_mid, w_out, radiation, fall_rate, active):
    fields, levels, columns = state.shape
    hid = w_in.shape[0]
    assert fields == NF and columns == 2 * LANES and hid == LANES and levels == 16
    share = -(-(hid + 24) // (8 * nz)) * 8
    cells = levels * hid
    wide = NF * levels
    chunk = (4, NF, levels, LANES)
    two = (2, NF, levels, LANES)
    dma = pltpu.SemaphoreType.DMA
    vmem = pltpu.VMEM
    scratch = [
        vmem(state.shape, F32),
        vmem(state.shape, F32),
        vmem((2 * NF, hid), BF16),
        vmem((hid, hid), BF16),
        vmem((NF, hid), BF16),
        vmem(radiation.shape, F32),
        vmem((1, columns), F32),
        vmem((1, columns), active.dtype),
        vmem((levels * 16, 2 * wide), BF16),
        vmem((levels * 16, wide), BF16),
        vmem((4,) + chunk, F32),
        vmem((4,) + chunk, F32),
        vmem((3,) + chunk, F32),
        vmem((3, nz, levels + 8, columns), F32),
        vmem((3, nz, levels + 8, columns), F32),
        vmem((3,) + two, F32),
        vmem((3,) + two, F32),
        vmem(two, F32),
        vmem((3, 2 * wide, columns), BF16),
        vmem((wide, columns), BF16),
        vmem((3, cells, columns), F32),
        vmem((3, cells, columns), F32),
        vmem((3, cells, columns), BF16),
        vmem((3, cells, columns), BF16),
        vmem((cells, 2 * wide), BF16),
        vmem((2 * wide, cells), BF16),
        vmem((wide, cells), BF16),
        vmem((cells, wide), BF16),
        vmem((hid, hid), BF16),
        vmem((cells, columns), BF16),
        vmem((cells, columns), BF16),
        vmem((levels * 16, columns), BF16),
        vmem((levels * 16, columns), BF16),
        vmem(radiation.shape, F32),
        vmem((9, levels, columns), F32),
        vmem(two, F32),
        vmem(two, F32),
        vmem((16, hid), F32),
        vmem((16, hid), F32),
        vmem((hid, hid), F32),
        vmem((nz, share, LANES), F32),
        vmem((nz, share, LANES), F32),
        vmem((nx, share, LANES), F32),
        vmem((nz * share, LANES), F32),
        dma((8,)), dma((7,)),
        dma((3, 3, 2)), dma((3, 3, 2)),
        dma((2, 3, nz)), dma((2, 3, nz)),
        dma((nz,)), dma((nz,)),
        dma((nx,)), dma((nx,)),
        dma((nz,)), dma((nz,)),
    ]
    results = pl.pallas_call(
        functools.partial(kernel, nz, nx, levels, hid, share),
        out_shape=(
            jax.ShapeDtypeStruct(state.shape, F32),
            jax.ShapeDtypeStruct(state.shape, F32),
            jax.ShapeDtypeStruct((hid, hid), F32),
            jax.ShapeDtypeStruct((2 * NF, hid), F32),
            jax.ShapeDtypeStruct((NF, hid), F32),
        ),
        in_specs=[pl.BlockSpec(memory_space=pl.ANY)] * 8,
        out_specs=[pl.BlockSpec(memory_space=pl.ANY)] * 5,
        scratch_shapes=scratch,
        compiler_params=pltpu.CompilerParams(
            collective_id=0, has_side_effects=True, vmem_limit_bytes=56 * 1024 * 1024
        ),
        name="adjoint_step",
    )(
        state, state_cot, w_in.T, w_mid, w_out, radiation,
        fall_rate.reshape(1, columns), active.reshape(1, columns),
    )
    new_state, state_grad, g_mid, g_in, g_out = pl.pallas_call(
        write_out,
        out_shape=tuple(jax.ShapeDtypeStruct(r.shape, r.dtype) for r in results),
        in_specs=[pl.BlockSpec(memory_space=pl.ANY)] * 5,
        out_specs=[pl.BlockSpec(memory_space=pl.ANY)] * 5,
        scratch_shapes=[dma((5,))],
        compiler_params=pltpu.CompilerParams(vmem_limit_bytes=56 * 1024 * 1024),
        name="write_out",
    )(*results)
    return new_state, state_grad, g_in.T, g_mid, g_out


def solution(mesh):
    placed = (P(None, "gz", "gx"), P(None, "gz", "gx"), P(), P(), P(), P(), P("gx"), P("gx"))
    return jax.shard_map(
        functools.partial(on_device, mesh.shape["gz"], mesh.shape["gx"]),
        mesh=mesh,
        in_specs=placed,
        out_specs=(P(None, "gz", "gx"), P(None, "gz", "gx"), P(), P(), P()),
        check_vma=False,
    )
```

```python
import functools

import jax
import jax.numpy as jnp
from jax import lax
from jax.experimental import pallas as pl
from jax.experimental.pallas import tpu as pltpu
from jax.sharding import PartitionSpec as P

NF = 6
NY = 64
LANES = 128
HALF = 8
HALF_BITS = 3
MESH = pl.DeviceIdType.MESH
F32 = jnp.float32
BF16 = jnp.bfloat16


def mm(a, b, precision=None):
    return lax.dot_general(
        a, b, (((1,), (0,)), ((), ())), precision=precision, preferred_element_type=F32
    )


def mm_t(a, b, precision=None):
    return lax.dot_general(
        a, b, (((1,), (1,)), ((), ())), precision=precision, preferred_element_type=F32
    )


def iota(shape, dim):
    return lax.broadcasted_iota(jnp.int32, shape, dim)


def kernel(
    nz, nx, levels, hid, share,
    state_hbm, cot_hbm, w_in_hbm, w_mid_hbm, w_out_hbm, rad_hbm, fall_hbm, act_hbm,
    new_state, state_grad, g_mid, g_in, g_out,
    state, cot, w_in, w_mid, w_out, rad, fall, act, pick_in, pick_out,
    sp, lp, gp, rim_out, rim_in, fallv, tg, tl, dxs, dys, moved, feats, out_cot, t1s, t2s, h1s, h2s,
    k1, k1t, k2, k2t, wmt, pre1, pre2, by_in, by_out, radt, tab, fcs, acc, a_in, a_out, a_mid,
    pack, part, parts, full,
    load_sem, store_sem, halo_send, halo_recv, gz_send, gz_recv, rs_send, rs_recv, ag_send, ag_recv, fin_send, fin_recv,
):
    mz, mx = lax.axis_index("gz"), lax.axis_index("gx")
    left, right = lax.rem(mx + nx - 1, nx), lax.rem(mx + 1, nx)

    barrier = pltpu.get_barrier_semaphore()
    for o in range(1, nz):
        pl.semaphore_signal(
            barrier, inc=1, device_id=(lax.rem(mz + o, nz), mx), device_id_type=MESH
        )
    for o in range(1, nx):
        pl.semaphore_signal(
            barrier, inc=1, device_id=(mz, lax.rem(mx + o, nx)), device_id_type=MESH
        )

    loads = [
        pltpu.make_async_copy(src, dst, load_sem.at[at])
        for at, (src, dst) in enumerate(
            [
                (state_hbm, state), (cot_hbm, cot), (w_in_hbm, w_in), (w_mid_hbm, w_mid),
                (w_out_hbm, w_out), (rad_hbm, rad), (fall_hbm, fall), (act_hbm, act),
            ]
        )
    ]
    for copy in loads:
        copy.start()
    a_in[...] = jnp.zeros_like(a_in)
    a_out[...] = jnp.zeros_like(a_out)
    a_mid[...] = jnp.zeros_like(a_mid)
    for copy in loads:
        copy.wait()

    columns = 2 * LANES
    shape = (levels, columns)
    rate = jnp.broadcast_to(fall[...], shape)
    r1 = rate / (1.0 + rate)
    r2 = r1 * r1
    r4 = r2 * r2
    r8 = r4 * r4
    powers = [r1, r2, r4, r8, r8 * r8]
    up, down = jnp.ones(shape, F32), jnp.ones(shape, F32)
    level = iota(shape, 0)
    for bit in range(5):
        up = jnp.where(((level + 1) >> bit) & 1 == 1, up * powers[bit], up)
        down = jnp.where(((levels - level) >> bit) & 1 == 1, down * powers[bit], down)
    for at, value in enumerate(
        powers + [1.0 / (1.0 + rate), jnp.broadcast_to(act[...].astype(F32), shape), down, up]
    ):
        tab[at] = value

    for c in range(2):
        lanes = slice(c * LANES, (c + 1) * LANES)
        sp[0, c + 1] = state[:, :, lanes]
        lp[0, c] = (2.0 / 3.0) * cot[:, :, lanes]
        acc[c] = cot[:, :, lanes] * (1.0 / 3.0)

    def rows_of(half):
        return pl.ds(pl.multiple_of(half * HALF, HALF), HALF)

    def sides(sources, targets, kind, k, half):
        return [
            pltpu.make_async_remote_copy(
                src_ref=sources[side].at[:, rows_of(half), :],
                dst_ref=targets[side].at[:, rows_of(half), :],
                send_sem=halo_send.at[kind, k, half, side],
                recv_sem=halo_recv.at[kind, k, half, side],
                device_id=(mz, (left, right)[side]), device_id_type=MESH,
            )
            for side in range(2)
        ]

    def halo(k, half):
        return sides((sp.at[k, 1], sp.at[k, 2]), (sp.at[k, 3], sp.at[k, 0]), 0, k, half)

    def rims(i, half):
        return sides((rim_out.at[i, 0], rim_out.at[i, 1]), (rim_in.at[i, 1], rim_in.at[i, 0]), 1, i, half)

    pl.semaphore_wait(barrier, nz - 1 + nx - 1)
    for half in range(2):
        for copy in halo(0, half):
            copy.start()

    def level_copies(buf, kind, k):
        sends, receives = [], []
        for o in range(1, nz):
            peer, source = lax.rem(mz + o, nz), lax.rem(mz + nz - o, nz)
            for dst, to in ((mz, sends), (source, receives)):
                to.append(
                    pltpu.make_async_remote_copy(
                        src_ref=buf.at[k, mz], dst_ref=buf.at[k, dst],
                        send_sem=gz_send.at[kind, k, o], recv_sem=gz_recv.at[kind, k, dst],
                        device_id=(peer, mx), device_id_type=MESH,
                    )
                )
        return sends, receives

    lane = iota((1, 1, LANES), 2)
    low = lane < NY
    y_last, y_first = lane & (NY - 1) == NY - 1, lane & (NY - 1) == 0
    depth = iota((levels, LANES), 0)

    def along_x(chunks):
        turned = [pltpu.roll(chunk, NY, 2) for chunk in chunks]
        out = []
        for i in (1, 2):
            plus = jnp.where(low, turned[i], turned[i + 1])
            minus = jnp.where(low, turned[i - 1], turned[i])
            out.append((plus, minus, (8.0 * (plus - minus) - (chunks[i + 1] - chunks[i - 1])) * (1.0 / 12.0)))
        return out

    def along_y(chunk):
        plus = jnp.where(y_last, pltpu.roll(chunk, NY - 1, 2), pltpu.roll(chunk, LANES - 1, 2))
        minus = jnp.where(y_first, pltpu.roll(chunk, NY + 1, 2), pltpu.roll(chunk, 1, 2))
        return plus, minus

    def settle(source, lanes, downward):
        value = tab[5, :, lanes] * source
        for bit in range(4):
            step = 1 << bit
            if downward:
                moved_by = pltpu.roll(value, levels - step, 0)
                inside = depth < levels - step
            else:
                moved_by = pltpu.roll(value, step, 0)
                inside = depth >= step
            value = value + tab[bit, :, lanes] * jnp.where(inside, moved_by, 0.0)
        return value

    def inflow(buf, k, lanes, downward):
        total = jnp.zeros((8, LANES), F32)
        order = range(nz - 1, 0, -1) if downward else range(nz - 1)
        for j in order:
            reached = j > mz if downward else j < mz
            following = buf[k, j, levels:, lanes] + tab[4, 0:8, lanes] * total
            total = jnp.where(reached, following, total)
        return total[0:1]

    def chunk_lanes(c):
        return slice(c * LANES, (c + 1) * LANES)

    def share_levels(k):
        for c in range(2):
            lanes = chunk_lanes(c)
            value = settle(sp[k, c + 1, 5], lanes, True)
            fallv[c, 0] = value
            tg[k, mz, 0:levels, lanes] = sp[k, c + 1, 3]
            tg[k, mz, levels:, lanes] = jnp.broadcast_to(value[0:1], (8, LANES))
        for copy in level_copies(tg, 0, k)[0]:
            copy.start()

    share_levels(0)

    def spread_t(rows, cols):
        return (iota((rows, cols), 0) >> HALF_BITS == iota((rows, cols), 1)).astype(F32).astype(BF16)

    eye = (iota((hid, hid), 0) == iota((hid, hid), 1)).astype(F32).astype(BF16)
    w1t = mm(spread_t(2 * NF * HALF, 2 * NF), w_in[...])
    w1 = mm_t(eye, w1t.astype(BF16))
    w2 = mm(spread_t(NF * HALF, NF), w_out[...])
    w2t = mm_t(eye, w2.astype(BF16))
    wmt[...] = mm_t(eye, w_mid[...]).astype(BF16)

    def place(z, carry):
        rows = pl.ds(pl.multiple_of(z * hid, hid), hid)
        k1[rows, :] = jnp.where(iota(w1.shape, 1) & (HALF - 1) == z, w1, 0.0).astype(BF16)
        k2t[rows, :] = jnp.where(iota(w2t.shape, 1) & (HALF - 1) == z, w2t, 0.0).astype(BF16)
        k1t[:, rows] = jnp.where(iota(w1t.shape, 0) & (HALF - 1) == z, w1t, 0.0).astype(BF16)
        k2[:, rows] = jnp.where(iota(w2.shape, 0) & (HALF - 1) == z, w2, 0.0).astype(BF16)
        return carry

    lax.fori_loop(0, HALF, place, 0)
    radt[...] = rad[...].T

    def gathered(cols):
        at = iota((HALF * 16, cols), 0)
        return ((at & 15) * HALF + (at >> 4) == iota((HALF * 16, cols), 1)).astype(F32).astype(BF16)

    pick_in[...] = gathered(2 * NF * HALF)
    pick_out[...] = gathered(NF * HALF)


    def forward(t, carry):
        k, half = t >> 1, t & 1
        rows8 = rows_of(half)
        own = [sp[k, 1, :, rows8, :], sp[k, 2, :, rows8, :]]
        for copy in halo(k, half):
            copy.wait_recv()
        x_sides = along_x([sp[k, 0, :, rows8, :], own[0], own[1], sp[k, 3, :, rows8, :]])
        for c in range(2):
            y_plus, y_minus = along_y(own[c])
            x_plus, x_minus, deriv_x = x_sides[c]
            deriv_y = (y_plus - y_minus) * 0.5
            laplace = x_plus + x_minus + y_plus + y_minus - 4.0 * own[c]
            dxs[k, c, :, rows8, :] = deriv_x
            dys[k, c, :, rows8, :] = deriv_y
            moved[c] = -(own[c][0:1] * deriv_x + own[c][1:2] * deriv_y) + 0.1 * laplace
            feats[k, half, 0 : NF * HALF, chunk_lanes(c)] = (
                own[c].reshape(NF * HALF, LANES).astype(BF16)
            )
            feats[k, half, NF * HALF :, chunk_lanes(c)] = (
                deriv_x.reshape(NF * HALF, LANES).astype(BF16)
            )

        def layers(group, inner):
            block = pl.ds(pl.multiple_of(group * (4 * hid), 4 * hid), 4 * hid)
            first = half * (HALF * hid) + group * (4 * hid)
            kept = pl.ds(pl.multiple_of(first, 4 * hid), 4 * hid)
            t1 = jnp.tanh(mm(k1[block, :], feats[k, half]))
            t1s[k, kept, :] = t1
            h1 = t1.astype(BF16)
            h1s[k, kept, :] = h1
            for j in range(4):
                rows = pl.ds(pl.multiple_of(first + j * hid, hid), hid)
                t2 = jnp.tanh(mm(w_mid[...], h1[j * hid : (j + 1) * hid]))
                t2s[k, rows, :] = t2
                h2s[k, rows, :] = t2.astype(BF16)
            return inner

        lax.fori_loop(0, HALF // 4, layers, 0)
        half_cells = pl.ds(pl.multiple_of(half * (HALF * hid), HALF * hid), HALF * hid)
        closure = mm(k2[...], h2s[k, half_cells, :])

        @pl.when(half == 0)
        def _():
            for copy in level_copies(tg, 0, k)[1]:
                copy.wait_recv()

        heat = mm(
            rad[pl.ds(pl.multiple_of(mz * levels + half * HALF, HALF), HALF), :],
            tg[k, :, 0:levels, :].reshape(nz * levels, columns),
            lax.Precision.HIGHEST,
        )
        keep = jnp.where(k == 0, 0.0, jnp.where(k == 1, 0.75, 1.0 / 3.0))
        take = jnp.where(k == 0, 1.0, jnp.where(k == 1, 0.25, 2.0 / 3.0))
        for c in range(2):
            lanes = chunk_lanes(c)
            total = moved[c] + closure[:, lanes].reshape(NF, HALF, LANES)
            fallen = fallv[c, 0, rows8, :] + tab[7, rows8, lanes] * inflow(tg, k, lanes, True)
            total = jnp.concatenate(
                [
                    total[0:3],
                    total[3:4] + heat[:, lanes][None],
                    total[4:5],
                    total[5:6] + (tab[6, rows8, lanes] * (fallen - own[c][5]))[None],
                ],
                0,
            )
            sp[k + 1, c + 1, :, rows8, :] = (
                keep * state[:, rows8, lanes] + take * (own[c] + 0.25 * total)
            )

        @pl.when(k < 2)
        def _():
            for copy in halo(k + 1, half):
                copy.start()

            @pl.when(half == 1)
            def _():
                share_levels(k + 1)

        return carry

    lax.fori_loop(0, 6, forward, 0)
    stores = []
    for c in range(2):
        stores.append(
            pltpu.make_async_copy(
                sp.at[3, c + 1], new_state.at[:, :, chunk_lanes(c)], store_sem.at[c]
            )
        )
        stores[-1].start()


    total_rows = nz * share
    scatter = []
    for o in range(1, nz):
        peer = lax.rem(mz + o, nz)
        scatter.append(
            pltpu.make_async_remote_copy(
                src_ref=pack.at[peer], dst_ref=part.at[o],
                send_sem=rs_send.at[o], recv_sem=rs_recv.at[o],
                device_id=(peer, mx), device_id_type=MESH,
            )
        )

    def backward(i, carry):
        k = 2 - i
        lam = [lp[i, 0], lp[i, 1]]
        local, masked = [], []
        for c in range(2):
            lanes = chunk_lanes(c)
            source = tab[6, :, lanes] * lam[c][5]
            value = settle(source, lanes, False)
            masked.append(source)
            local.append(value)
            tl[i, mz, 0:levels, lanes] = lam[c][3]
            tl[i, mz, levels:, lanes] = jnp.broadcast_to(value[levels - 1 : levels], (8, LANES))
            for half in range(2):
                out_cot[half, :, lanes] = (
                    lam[c][:, half * HALF : (half + 1) * HALF, :]
                    .reshape(NF * HALF, LANES).astype(BF16)
                )
        sends, receives = level_copies(tl, 1, i)
        for copy in sends:
            copy.start()

        def by_half(half, outer):
            rows8 = rows_of(half)

            def layers(group, inner):
                block = pl.ds(pl.multiple_of(group * (4 * hid), 4 * hid), 4 * hid)
                first = half * (HALF * hid) + group * (4 * hid)
                kept = pl.ds(pl.multiple_of(first, 4 * hid), 4 * hid)
                t2 = t2s[k, kept, :]
                p2 = (mm(k2t[block, :], out_cot[half]) * (1.0 - t2 * t2)).astype(BF16)
                pre2[kept, :] = p2
                for j in range(4):
                    rows = pl.ds(pl.multiple_of(first + j * hid, hid), hid)
                    t1 = t1s[k, rows, :]
                    back = mm(wmt[...], p2[j * hid : (j + 1) * hid])
                    pre1[rows, :] = (back * (1.0 - t1 * t1)).astype(BF16)
                return inner

            lax.fori_loop(0, HALF // 4, layers, 0)
            half_cells = pl.ds(pl.multiple_of(half * (HALF * hid), HALF * hid), HALF * hid)
            feature_cot = mm(k1t[...], pre1[half_cells, :])
            for c in range(2):
                lanes = chunk_lanes(c)
                fcs[c, :, rows8, :] = feature_cot[0 : NF * HALF, lanes].reshape(NF, HALF, LANES)
                now = lp[i, c, :, rows8, :]
                source = (
                    feature_cot[NF * HALF :, lanes].reshape(NF, HALF, LANES)
                    - sp[k, c + 1, 0:1, rows8, :] * now
                )
                gp[c, :, rows8, :] = source
                turned = pltpu.roll(source, NY, 2)
                spread_lam = 0.1 * pltpu.roll(now, NY, 2)
                if c == 0:
                    near = (source - 8.0 * turned) * (1.0 / 12.0) + spread_lam
                    rim_out[i, 0, :, rows8, :] = jnp.where(low, source * (1.0 / 12.0), near)
                else:
                    near = (8.0 * turned - source) * (1.0 / 12.0) + spread_lam
                    rim_out[i, 1, :, rows8, :] = jnp.where(low, near, source * (-1.0 / 12.0))
            for copy in rims(i, half):
                copy.start()
            few = pl.ds(pl.multiple_of(half * (HALF * 16), HALF * 16), HALF * 16)
            by_in[few, :] = mm(pick_in[...], feats[k, half]).astype(BF16)
            by_out[few, :] = mm(pick_out[...], out_cot[half]).astype(BF16)
            return outer

        lax.fori_loop(0, 2, by_half, 0)

        def terms(group, inner):
            s_in, s_out, s_mid = inner
            for j in range(4):
                z = group * 4 + j
                rows = pl.ds(pl.multiple_of(z * hid, hid), hid)
                few = pl.ds(pl.multiple_of(z * 16, 16), 16)
                s_mid = s_mid + mm_t(pre2[rows, :], h1s[k, rows, :])
                s_in = s_in + mm_t(by_in[few, :], pre1[rows, :])
                s_out = s_out + mm_t(by_out[few, :], h2s[k, rows, :])
            return s_in, s_out, s_mid

        s_in, s_out, s_mid = lax.fori_loop(
            0, levels // 4, terms, (a_in[...], a_out[...], a_mid[...])
        )
        a_in[...] = s_in
        a_out[...] = s_out
        a_mid[...] = s_mid

        @pl.when(k == 0)
        def _():
            everything = jnp.concatenate(
                [
                    a_mid[...],
                    a_in[...],
                    a_out[0:8, :],
                    jnp.zeros((total_rows - hid - 24, LANES), F32),
                ],
                0,
            )
            pack[...] = everything.reshape(nz, share, LANES)
            for copy in scatter:
                copy.start()

        for copy in receives:
            copy.wait_recv()
        heat = mm(
            radt[pl.ds(pl.multiple_of(mz * levels, levels), levels), :],
            tl[i, :, 0:levels, :].reshape(nz * levels, columns),
            lax.Precision.HIGHEST,
        )
        zero = jnp.zeros((NF, levels, LANES), F32)
        lam_sides = along_x([zero, lam[0], lam[1], zero])
        g_sides = along_x([zero, gp[0], gp[1], zero])
        for half in range(2):
            for copy in rims(i, half):
                copy.wait_recv()
        weight = jnp.where(k == 0, 1.0, jnp.where(k == 1, 0.0, 0.75))
        share_on = jnp.where(k == 2, 0.25, 1.0)
        for c in range(2):
            lanes = chunk_lanes(c)
            now = lam[c]
            y_plus, y_minus = along_y(now)
            x_plus, x_minus, _ = lam_sides[c]
            carried_plus, carried_minus = along_y(sp[k, c + 1, 1:2] * now)
            back = (
                (carried_plus - carried_minus) * 0.5
                - g_sides[c][2]
                + 0.1 * (x_plus + x_minus + y_plus + y_minus - 4.0 * now)
                + fcs[c]
                + rim_in[i, c]
            )
            pulled = local[c] + tab[8, :, lanes] * inflow(tl, i, lanes, False)
            back = jnp.concatenate(
                [
                    back[0:1] - jnp.sum(now * dxs[k, c], axis=0, keepdims=True),
                    back[1:2] - jnp.sum(now * dys[k, c], axis=0, keepdims=True),
                    back[2:3],
                    back[3:4] + heat[:, lanes][None],
                    back[4:5],
                    back[5:6] + (pulled - masked[c])[None],
                ],
                0,
            )
            whole = now + 0.25 * back
            acc[c] = acc[c] + weight * whole
            lp[i + 1, c] = share_on * whole
        return carry

    lax.fori_loop(0, 3, backward, 0)
    for c in range(2):
        stores.append(
            pltpu.make_async_copy(
                acc.at[c], state_grad.at[:, :, chunk_lanes(c)], store_sem.at[2 + c]
            )
        )
        stores[-1].start()

    mine = pack[mz]
    for o in range(1, nz):
        scatter[o - 1].wait_recv()
        mine = mine + part[o]
    parts[mx] = mine

    sends, receives = [], []
    for o in range(1, nx):
        peer, source = lax.rem(mx + o, nx), lax.rem(mx + nx - o, nx)
        for dst, to in ((mx, sends), (source, receives)):
            to.append(
                pltpu.make_async_remote_copy(
                    src_ref=parts.at[mx], dst_ref=parts.at[dst],
                    send_sem=ag_send.at[o], recv_sem=ag_recv.at[dst],
                    device_id=(mz, peer), device_id_type=MESH,
                )
            )
    for copy in sends:
        copy.start()
    for copy in receives:
        copy.wait_recv()
    summed = parts[0]
    for j in range(1, nx):
        summed = summed + parts[j]

    def quarter(index):
        return pl.ds(pl.multiple_of(index * share, 8), share)

    full[quarter(mz), :] = 0.25 * summed

    sends_z, receives_z = [], []
    for o in range(1, nz):
        peer, source = lax.rem(mz + o, nz), lax.rem(mz + nz - o, nz)
        for dst, to in ((mz, sends_z), (source, receives_z)):
            to.append(
                pltpu.make_async_remote_copy(
                    src_ref=full.at[quarter(mz)], dst_ref=full.at[quarter(dst)],
                    send_sem=fin_send.at[o], recv_sem=fin_recv.at[dst],
                    device_id=(peer, mx), device_id_type=MESH,
                )
            )
    for copy in sends_z:
        copy.start()
    for copy in receives_z:
        copy.wait_recv()
    for at, (out, first, count) in enumerate(
        ((g_mid, 0, hid), (g_in, hid, 2 * NF), (g_out, hid + 16, NF))
    ):
        stores.append(
            pltpu.make_async_copy(full.at[first : first + count], out, store_sem.at[4 + at])
        )
        stores[-1].start()
    for copy in stores:
        copy.wait()
    for k in range(3):
        for half in range(2):
            for copy in halo(k, half) + rims(k, half):
                copy.wait_send()
        for copy in level_copies(tg, 0, k)[0] + level_copies(tl, 1, k)[0]:
            copy.wait_send()
    for copy in scatter + sends + sends_z:
        copy.wait_send()


def write_out(*refs):
    sources, outs, held, sems = refs[:5], refs[5:10], refs[10:15], refs[15]
    loads = [pltpu.make_async_copy(sources[at], held[at], sems.at[0, at]) for at in range(5)]
    stores = [pltpu.make_async_copy(held[at], outs[at], sems.at[1, at]) for at in range(5)]
    for copy in loads:
        copy.start()
    for load, store in zip(loads, stores):
        load.wait()
        store.start()
    for copy in stores:
        copy.wait()


def on_device(nz, nx, state, state_cot, w_in, w_mid, w_out, radiation, fall_rate, active):
    fields, levels, columns = state.shape
    hid = w_in.shape[0]
    assert fields == NF and columns == 2 * LANES and hid == LANES and levels == 16
    share = -(-(hid + 24) // (8 * nz)) * 8
    cells = levels * hid
    wide = NF * HALF
    chunk = (4, NF, levels, LANES)
    two = (2, NF, levels, LANES)
    dma = pltpu.SemaphoreType.DMA
    vmem = pltpu.VMEM
    scratch = [
        vmem(state.shape, F32),
        vmem(state.shape, F32),
        vmem((2 * NF, hid), BF16),
        vmem((hid, hid), BF16),
        vmem((NF, hid), BF16),
        vmem(radiation.shape, F32),
        vmem((1, columns), F32),
        vmem((1, columns), active.dtype),
        vmem((HALF * 16, 2 * wide), BF16),
        vmem((HALF * 16, wide), BF16),
        vmem((4,) + chunk, F32),
        vmem((4,) + two, F32),
        vmem(two, F32),
        vmem((3,) + two, F32),
        vmem((3,) + two, F32),
        vmem((2, 1, levels, LANES), F32),
        vmem((3, nz, levels + 8, columns), F32),
        vmem((3, nz, levels + 8, columns), F32),
        vmem((3,) + two, F32),
        vmem((3,) + two, F32),
        vmem((2, NF, HALF, LANES), F32),
        vmem((3, 2, 2 * wide, columns), BF16),
        vmem((2, wide, columns), BF16),
        vmem((3, cells, columns), F32),
        vmem((3, cells, columns), F32),
        vmem((3, cells, columns), BF16),
        vmem((3, cells, columns), BF16),
        vmem((cells // 2, 2 * wide), BF16),
        vmem((2 * wide, cells // 2), BF16),
        vmem((wide, cells // 2), BF16),
        vmem((cells // 2, wide), BF16),
        vmem((hid, hid), BF16),
        vmem((cells, columns), BF16),
        vmem((cells, columns), BF16),
        vmem((levels * 16, columns), BF16),
        vmem((levels * 16, columns), BF16),
        vmem(radiation.shape, F32),
        vmem((9, levels, columns), F32),
        vmem(two, F32),
        vmem(two, F32),
        vmem((16, hid), F32),
        vmem((16, hid), F32),
        vmem((hid, hid), F32),
        vmem((nz, share, LANES), F32),
        vmem((nz, share, LANES), F32),
        vmem((nx, share, LANES), F32),
        vmem((nz * share, LANES), F32),
        dma((8,)), dma((7,)),
        dma((2, 3, 2, 2)), dma((2, 3, 2, 2)),
        dma((2, 3, nz)), dma((2, 3, nz)),
        dma((nz,)), dma((nz,)),
        dma((nx,)), dma((nx,)),
        dma((nz,)), dma((nz,)),
    ]
    results = pl.pallas_call(
        functools.partial(kernel, nz, nx, levels, hid, share),
        out_shape=(
            jax.ShapeDtypeStruct(state.shape, F32),
            jax.ShapeDtypeStruct(state.shape, F32),
            jax.ShapeDtypeStruct((hid, hid), F32),
            jax.ShapeDtypeStruct((2 * NF, hid), F32),
            jax.ShapeDtypeStruct((NF, hid), F32),
        ),
        in_specs=[pl.BlockSpec(memory_space=pl.ANY)] * 8,
        out_specs=[pl.BlockSpec(memory_space=pl.ANY)] * 5,
        scratch_shapes=scratch,
        compiler_params=pltpu.CompilerParams(
            collective_id=0, has_side_effects=True, vmem_limit_bytes=56 * 1024 * 1024
        ),
        name="adjoint_step",
    )(
        state, state_cot, w_in.T, w_mid, w_out, radiation,
        fall_rate.reshape(1, columns), active.reshape(1, columns),
    )
    new_state, state_grad, g_mid, g_in, g_out = pl.pallas_call(
        write_out,
        out_shape=tuple(jax.ShapeDtypeStruct(r.shape, r.dtype) for r in results),
        in_specs=[pl.BlockSpec(memory_space=pl.ANY)] * 5,
        out_specs=[pl.BlockSpec(memory_space=pl.ANY)] * 5,
        scratch_shapes=[vmem(r.shape, r.dtype) for r in results] + [dma((2, 5))],
        compiler_params=pltpu.CompilerParams(vmem_limit_bytes=56 * 1024 * 1024),
        name="write_out",
    )(*results)
    return new_state, state_grad, g_in.T, g_mid, g_out


def solution(mesh):
    placed = (P(None, "gz", "gx"), P(None, "gz", "gx"), P(), P(), P(), P(), P("gx"), P("gx"))
    return jax.shard_map(
        functools.partial(on_device, mesh.shape["gz"], mesh.shape["gx"]),
        mesh=mesh,
        in_specs=placed,
        out_specs=(P(None, "gz", "gx"), P(None, "gz", "gx"), P(), P(), P()),
        check_vma=False,
    )
```

```python
import functools

import jax
import jax.numpy as jnp
from jax import lax
from jax.experimental import pallas as pl
from jax.experimental.pallas import tpu as pltpu
from jax.sharding import PartitionSpec as P

NF = 6
NY = 64
LANES = 128
HALF = 8
HALF_BITS = 3
MESH = pl.DeviceIdType.MESH
F32 = jnp.float32
BF16 = jnp.bfloat16


def mm(a, b, precision=None):
    return lax.dot_general(
        a, b, (((1,), (0,)), ((), ())), precision=precision, preferred_element_type=F32
    )


def mm_t(a, b, precision=None):
    return lax.dot_general(
        a, b, (((1,), (1,)), ((), ())), precision=precision, preferred_element_type=F32
    )


def iota(shape, dim):
    return lax.broadcasted_iota(jnp.int32, shape, dim)


def kernel(
    nz, nx, levels, hid, share,
    state_hbm, cot_hbm, w_in_hbm, w_mid_hbm, w_out_hbm, rad_hbm, fall_hbm, act_hbm,
    new_state, state_grad, g_mid, g_in, g_out,
    state, cot, w_in, w_mid, w_out, rad, fall, act,
    sp, lp, gp, rim_out, rim_in, fallv, tg, tl, dxs, dys, moved, feats, out_cot, t1s, t2s, h1s, h2s,
    k1, k1t, k2, k2t, wmt, pre1, pre2, radt, tab, fcs, acc, a_in, a_out, a_mid,
    pack, part, parts, full,
    load_sem, store_sem, halo_send, halo_recv, gz_send, gz_recv, rs_send, rs_recv, ag_send, ag_recv, fin_send, fin_recv,
):
    mz, mx = lax.axis_index("gz"), lax.axis_index("gx")
    left, right = lax.rem(mx + nx - 1, nx), lax.rem(mx + 1, nx)

    barrier = pltpu.get_barrier_semaphore()
    for o in range(1, nz):
        pl.semaphore_signal(
            barrier, inc=1, device_id=(lax.rem(mz + o, nz), mx), device_id_type=MESH
        )
    for o in range(1, nx):
        pl.semaphore_signal(
            barrier, inc=1, device_id=(mz, lax.rem(mx + o, nx)), device_id_type=MESH
        )

    loads = [
        pltpu.make_async_copy(src, dst, load_sem.at[at])
        for at, (src, dst) in enumerate(
            [
                (state_hbm, state), (cot_hbm, cot), (w_in_hbm, w_in), (w_mid_hbm, w_mid),
                (w_out_hbm, w_out), (rad_hbm, rad), (fall_hbm, fall), (act_hbm, act),
            ]
        )
    ]
    for copy in loads:
        copy.start()
    a_in[...] = jnp.zeros_like(a_in)
    a_out[...] = jnp.zeros_like(a_out)
    a_mid[...] = jnp.zeros_like(a_mid)
    for copy in loads:
        copy.wait()

    columns = 2 * LANES
    shape = (levels, columns)
    rate = jnp.broadcast_to(fall[...], shape)
    r1 = rate / (1.0 + rate)
    r2 = r1 * r1
    r4 = r2 * r2
    r8 = r4 * r4
    powers = [r1, r2, r4, r8, r8 * r8]
    up, down = jnp.ones(shape, F32), jnp.ones(shape, F32)
    level = iota(shape, 0)
    for bit in range(5):
        up = jnp.where(((level + 1) >> bit) & 1 == 1, up * powers[bit], up)
        down = jnp.where(((levels - level) >> bit) & 1 == 1, down * powers[bit], down)
    for at, value in enumerate(
        powers + [1.0 / (1.0 + rate), jnp.broadcast_to(act[...].astype(F32), shape), down, up]
    ):
        tab[at] = value

    for c in range(2):
        lanes = slice(c * LANES, (c + 1) * LANES)
        sp[0, c + 1] = state[:, :, lanes]
        lp[0, c] = (2.0 / 3.0) * cot[:, :, lanes]
        acc[c] = cot[:, :, lanes] * (1.0 / 3.0)

    def rows_of(half):
        return pl.ds(pl.multiple_of(half * HALF, HALF), HALF)

    def sides(sources, targets, kind, k, half):
        return [
            pltpu.make_async_remote_copy(
                src_ref=sources[side].at[:, rows_of(half), :],
                dst_ref=targets[side].at[:, rows_of(half), :],
                send_sem=halo_send.at[kind, k, half, side],
                recv_sem=halo_recv.at[kind, k, half, side],
                device_id=(mz, (left, right)[side]), device_id_type=MESH,
            )
            for side in range(2)
        ]

    def halo(k, half):
        return sides((sp.at[k, 1], sp.at[k, 2]), (sp.at[k, 3], sp.at[k, 0]), 0, k, half)

    def rims(i, half):
        return sides((rim_out.at[i, 0], rim_out.at[i, 1]), (rim_in.at[i, 1], rim_in.at[i, 0]), 1, i, half)

    pl.semaphore_wait(barrier, nz - 1 + nx - 1)
    for half in range(2):
        for copy in halo(0, half):
            copy.start()

    def level_copies(buf, kind, k):
        sends, receives = [], []
        for o in range(1, nz):
            peer, source = lax.rem(mz + o, nz), lax.rem(mz + nz - o, nz)
            for dst, to in ((mz, sends), (source, receives)):
                to.append(
                    pltpu.make_async_remote_copy(
                        src_ref=buf.at[k, mz], dst_ref=buf.at[k, dst],
                        send_sem=gz_send.at[kind, k, o], recv_sem=gz_recv.at[kind, k, dst],
                        device_id=(peer, mx), device_id_type=MESH,
                    )
                )
        return sends, receives

    lane = iota((1, 1, LANES), 2)
    low = lane < NY
    y_last, y_first = lane & (NY - 1) == NY - 1, lane & (NY - 1) == 0
    depth = iota((levels, LANES), 0)

    def along_x(chunks):
        turned = [pltpu.roll(chunk, NY, 2) for chunk in chunks]
        out = []
        for i in (1, 2):
            plus = jnp.where(low, turned[i], turned[i + 1])
            minus = jnp.where(low, turned[i - 1], turned[i])
            out.append((plus, minus, (8.0 * (plus - minus) - (chunks[i + 1] - chunks[i - 1])) * (1.0 / 12.0)))
        return out

    def along_y(chunk):
        plus = jnp.where(y_last, pltpu.roll(chunk, NY - 1, 2), pltpu.roll(chunk, LANES - 1, 2))
        minus = jnp.where(y_first, pltpu.roll(chunk, NY + 1, 2), pltpu.roll(chunk, 1, 2))
        return plus, minus

    def settle(source, lanes, downward):
        value = tab[5, :, lanes] * source
        for bit in range(4):
            step = 1 << bit
            if downward:
                moved_by = pltpu.roll(value, levels - step, 0)
                inside = depth < levels - step
            else:
                moved_by = pltpu.roll(value, step, 0)
                inside = depth >= step
            value = value + tab[bit, :, lanes] * jnp.where(inside, moved_by, 0.0)
        return value

    def inflow(buf, k, lanes, downward):
        total = jnp.zeros((8, LANES), F32)
        order = range(nz - 1, 0, -1) if downward else range(nz - 1)
        for j in order:
            reached = j > mz if downward else j < mz
            following = buf[k, j, levels:, lanes] + tab[4, 0:8, lanes] * total
            total = jnp.where(reached, following, total)
        return total[0:1]

    def chunk_lanes(c):
        return slice(c * LANES, (c + 1) * LANES)

    def share_levels(k):
        for c in range(2):
            lanes = chunk_lanes(c)
            value = settle(sp[k, c + 1, 5], lanes, True)
            fallv[c, 0] = value
            tg[k, mz, 0:levels, lanes] = sp[k, c + 1, 3]
            tg[k, mz, levels:, lanes] = jnp.broadcast_to(value[0:1], (8, LANES))
        for copy in level_copies(tg, 0, k)[0]:
            copy.start()

    share_levels(0)

    def spread_t(rows, cols):
        return (iota((rows, cols), 0) >> HALF_BITS == iota((rows, cols), 1)).astype(F32).astype(BF16)

    eye = (iota((hid, hid), 0) == iota((hid, hid), 1)).astype(F32).astype(BF16)
    w1t = mm(spread_t(2 * NF * HALF, 2 * NF), w_in[...])
    w1 = mm_t(eye, w1t.astype(BF16))
    w2 = mm(spread_t(NF * HALF, NF), w_out[...])
    w2t = mm_t(eye, w2.astype(BF16))
    wmt[...] = mm_t(eye, w_mid[...]).astype(BF16)

    def place(z, carry):
        rows = pl.ds(pl.multiple_of(z * hid, hid), hid)
        k1[rows, :] = jnp.where(iota(w1.shape, 1) & (HALF - 1) == z, w1, 0.0).astype(BF16)
        k2t[rows, :] = jnp.where(iota(w2t.shape, 1) & (HALF - 1) == z, w2t, 0.0).astype(BF16)
        k1t[:, rows] = jnp.where(iota(w1t.shape, 0) & (HALF - 1) == z, w1t, 0.0).astype(BF16)
        k2[:, rows] = jnp.where(iota(w2.shape, 0) & (HALF - 1) == z, w2, 0.0).astype(BF16)
        return carry

    lax.fori_loop(0, HALF, place, 0)
    radt[...] = rad[...].T

    def forward(t, carry):
        k, half = t >> 1, t & 1
        rows8 = rows_of(half)
        own = [sp[k, 1, :, rows8, :], sp[k, 2, :, rows8, :]]
        for copy in halo(k, half):
            copy.wait_recv()
        x_sides = along_x([sp[k, 0, :, rows8, :], own[0], own[1], sp[k, 3, :, rows8, :]])
        for c in range(2):
            y_plus, y_minus = along_y(own[c])
            x_plus, x_minus, deriv_x = x_sides[c]
            deriv_y = (y_plus - y_minus) * 0.5
            laplace = x_plus + x_minus + y_plus + y_minus - 4.0 * own[c]
            dxs[k, c, :, rows8, :] = deriv_x
            dys[k, c, :, rows8, :] = deriv_y
            moved[c] = -(own[c][0:1] * deriv_x + own[c][1:2] * deriv_y) + 0.1 * laplace
            feats[k, half, 0 : NF * HALF, chunk_lanes(c)] = (
                own[c].reshape(NF * HALF, LANES).astype(BF16)
            )
            feats[k, half, NF * HALF :, chunk_lanes(c)] = (
                deriv_x.reshape(NF * HALF, LANES).astype(BF16)
            )

        def layers(group, inner):
            block = pl.ds(pl.multiple_of(group * (4 * hid), 4 * hid), 4 * hid)
            first = half * (HALF * hid) + group * (4 * hid)
            kept = pl.ds(pl.multiple_of(first, 4 * hid), 4 * hid)
            t1 = jnp.tanh(mm(k1[block, :], feats[k, half]))
            t1s[k, kept, :] = t1
            h1 = t1.astype(BF16)
            h1s[k, kept, :] = h1
            for j in range(4):
                rows = pl.ds(pl.multiple_of(first + j * hid, hid), hid)
                t2 = jnp.tanh(mm(w_mid[...], h1[j * hid : (j + 1) * hid]))
                t2s[k, rows, :] = t2
                h2s[k, rows, :] = t2.astype(BF16)
            return inner

        lax.fori_loop(0, HALF // 4, layers, 0)
        half_cells = pl.ds(pl.multiple_of(half * (HALF * hid), HALF * hid), HALF * hid)
        closure = mm(k2[...], h2s[k, half_cells, :])

        @pl.when(half == 0)
        def _():
            for copy in level_copies(tg, 0, k)[1]:
                copy.wait_recv()

        heat = mm(
            rad[pl.ds(pl.multiple_of(mz * levels + half * HALF, HALF), HALF), :],
            tg[k, :, 0:levels, :].reshape(nz * levels, columns),
            lax.Precision.HIGHEST,
        )
        keep = jnp.where(k == 0, 0.0, jnp.where(k == 1, 0.75, 1.0 / 3.0))
        take = jnp.where(k == 0, 1.0, jnp.where(k == 1, 0.25, 2.0 / 3.0))
        for c in range(2):
            lanes = chunk_lanes(c)
            total = moved[c] + closure[:, lanes].reshape(NF, HALF, LANES)
            fallen = fallv[c, 0, rows8, :] + tab[7, rows8, lanes] * inflow(tg, k, lanes, True)
            total = jnp.concatenate(
                [
                    total[0:3],
                    total[3:4] + heat[:, lanes][None],
                    total[4:5],
                    total[5:6] + (tab[6, rows8, lanes] * (fallen - own[c][5]))[None],
                ],
                0,
            )
            sp[k + 1, c + 1, :, rows8, :] = (
                keep * state[:, rows8, lanes] + take * (own[c] + 0.25 * total)
            )

        @pl.when(k < 2)
        def _():
            for copy in halo(k + 1, half):
                copy.start()

            @pl.when(half == 1)
            def _():
                share_levels(k + 1)

        return carry

    lax.fori_loop(0, 6, forward, 0)
    stores = []
    for c in range(2):
        stores.append(
            pltpu.make_async_copy(
                sp.at[3, c + 1], new_state.at[:, :, chunk_lanes(c)], store_sem.at[c]
            )
        )
        stores[-1].start()


    total_rows = nz * share
    scatter = []
    for o in range(1, nz):
        peer = lax.rem(mz + o, nz)
        scatter.append(
            pltpu.make_async_remote_copy(
                src_ref=pack.at[peer], dst_ref=part.at[o],
                send_sem=rs_send.at[o], recv_sem=rs_recv.at[o],
                device_id=(peer, mx), device_id_type=MESH,
            )
        )

    def fold(rows, cols):
        return (iota((rows, cols), 1) >> HALF_BITS == iota((rows, cols), 0)).astype(F32)

    def backward(i, carry):
        k = 2 - i
        lam = [lp[i, 0], lp[i, 1]]
        local, masked = [], []
        for c in range(2):
            lanes = chunk_lanes(c)
            source = tab[6, :, lanes] * lam[c][5]
            value = settle(source, lanes, False)
            masked.append(source)
            local.append(value)
            tl[i, mz, 0:levels, lanes] = lam[c][3]
            tl[i, mz, levels:, lanes] = jnp.broadcast_to(value[levels - 1 : levels], (8, LANES))
            for half in range(2):
                out_cot[half, :, lanes] = (
                    lam[c][:, half * HALF : (half + 1) * HALF, :]
                    .reshape(NF * HALF, LANES).astype(BF16)
                )
        sends, receives = level_copies(tl, 1, i)
        for copy in sends:
            copy.start()

        def by_half(half, outer):
            rows8 = rows_of(half)

            def layers(group, inner):
                block = pl.ds(pl.multiple_of(group * (4 * hid), 4 * hid), 4 * hid)
                first = half * (HALF * hid) + group * (4 * hid)
                kept = pl.ds(pl.multiple_of(first, 4 * hid), 4 * hid)
                t2 = t2s[k, kept, :]
                p2 = (mm(k2t[block, :], out_cot[half]) * (1.0 - t2 * t2)).astype(BF16)
                pre2[kept, :] = p2
                for j in range(4):
                    rows = pl.ds(pl.multiple_of(first + j * hid, hid), hid)
                    t1 = t1s[k, rows, :]
                    back = mm(wmt[...], p2[j * hid : (j + 1) * hid])
                    pre1[rows, :] = (back * (1.0 - t1 * t1)).astype(BF16)
                return inner

            lax.fori_loop(0, HALF // 4, layers, 0)
            half_cells = pl.ds(pl.multiple_of(half * (HALF * hid), HALF * hid), HALF * hid)
            feature_cot = mm(k1t[...], pre1[half_cells, :])
            for c in range(2):
                lanes = chunk_lanes(c)
                fcs[c, :, rows8, :] = feature_cot[0 : NF * HALF, lanes].reshape(NF, HALF, LANES)
                now = lp[i, c, :, rows8, :]
                source = (
                    feature_cot[NF * HALF :, lanes].reshape(NF, HALF, LANES)
                    - sp[k, c + 1, 0:1, rows8, :] * now
                )
                gp[c, :, rows8, :] = source
                turned = pltpu.roll(source, NY, 2)
                spread_lam = 0.1 * pltpu.roll(now, NY, 2)
                if c == 0:
                    near = (source - 8.0 * turned) * (1.0 / 12.0) + spread_lam
                    rim_out[i, 0, :, rows8, :] = jnp.where(low, source * (1.0 / 12.0), near)
                else:
                    near = (8.0 * turned - source) * (1.0 / 12.0) + spread_lam
                    rim_out[i, 1, :, rows8, :] = jnp.where(low, near, source * (-1.0 / 12.0))
            for copy in rims(i, half):
                copy.start()
            return outer

        lax.fori_loop(0, 2, by_half, 0)

        def terms(group, inner):
            s_in, s_out, s_mid = inner
            half = group >> 1
            block = pl.ds(pl.multiple_of(group * (4 * hid), 4 * hid), 4 * hid)
            for_in = mm_t(pre1[block, :], feats[k, half])
            for_out = mm_t(h2s[k, block, :], out_cot[half])
            for j in range(4):
                z = (group & 1) * 4 + j
                rows = pl.ds(pl.multiple_of((group * 4 + j) * hid, hid), hid)
                part_rows = slice(j * hid, (j + 1) * hid)
                s_mid = s_mid + mm_t(pre2[rows, :], h1s[k, rows, :])
                s_in = s_in + jnp.where(
                    iota(s_in.shape, 1) & (HALF - 1) == z, for_in[part_rows], 0.0
                )
                s_out = s_out + jnp.where(
                    iota(s_out.shape, 1) & (HALF - 1) == z, for_out[part_rows], 0.0
                )
            return s_in, s_out, s_mid

        s_in, s_out, s_mid = lax.fori_loop(
            0, levels // 4, terms, (a_in[...], a_out[...], a_mid[...])
        )
        a_in[...] = s_in
        a_out[...] = s_out
        a_mid[...] = s_mid

        @pl.when(k == 0)
        def _():
            everything = jnp.concatenate(
                [
                    a_mid[...],
                    mm_t(fold(16, 2 * NF * HALF), a_in[...], lax.Precision.HIGHEST),
                    mm_t(fold(8, NF * HALF), a_out[...], lax.Precision.HIGHEST),
                    jnp.zeros((total_rows - hid - 24, LANES), F32),
                ],
                0,
            )
            pack[...] = everything.reshape(nz, share, LANES)
            for copy in scatter:
                copy.start()

        for copy in receives:
            copy.wait_recv()
        heat = mm(
            radt[pl.ds(pl.multiple_of(mz * levels, levels), levels), :],
            tl[i, :, 0:levels, :].reshape(nz * levels, columns),
            lax.Precision.HIGHEST,
        )
        zero = jnp.zeros((NF, levels, LANES), F32)
        lam_sides = along_x([zero, lam[0], lam[1], zero])
        g_sides = along_x([zero, gp[0], gp[1], zero])
        for half in range(2):
            for copy in rims(i, half):
                copy.wait_recv()
        weight = jnp.where(k == 0, 1.0, jnp.where(k == 1, 0.0, 0.75))
        share_on = jnp.where(k == 2, 0.25, 1.0)
        for c in range(2):
            lanes = chunk_lanes(c)
            now = lam[c]
            y_plus, y_minus = along_y(now)
            x_plus, x_minus, _ = lam_sides[c]
            carried_plus, carried_minus = along_y(sp[k, c + 1, 1:2] * now)
            back = (
                (carried_plus - carried_minus) * 0.5
                - g_sides[c][2]
                + 0.1 * (x_plus + x_minus + y_plus + y_minus - 4.0 * now)
                + fcs[c]
                + rim_in[i, c]
            )
            pulled = local[c] + tab[8, :, lanes] * inflow(tl, i, lanes, False)
            back = jnp.concatenate(
                [
                    back[0:1] - jnp.sum(now * dxs[k, c], axis=0, keepdims=True),
                    back[1:2] - jnp.sum(now * dys[k, c], axis=0, keepdims=True),
                    back[2:3],
                    back[3:4] + heat[:, lanes][None],
                    back[4:5],
                    back[5:6] + (pulled - masked[c])[None],
                ],
                0,
            )
            whole = now + 0.25 * back
            acc[c] = acc[c] + weight * whole
            lp[i + 1, c] = share_on * whole
        return carry

    lax.fori_loop(0, 3, backward, 0)
    for c in range(2):
        stores.append(
            pltpu.make_async_copy(
                acc.at[c], state_grad.at[:, :, chunk_lanes(c)], store_sem.at[2 + c]
            )
        )
        stores[-1].start()

    mine = pack[mz]
    for o in range(1, nz):
        scatter[o - 1].wait_recv()
        mine = mine + part[o]
    sends = []
    summed = mine
    for at in range(nx.bit_length() - 1):
        step = 1 << at
        partner = mx + step - 2 * step * lax.rem(lax.div(mx, step), 2)
        parts[at, 0] = summed
        sends.append(
            pltpu.make_async_remote_copy(
                src_ref=parts.at[at, 0], dst_ref=parts.at[at, 1],
                send_sem=ag_send.at[at], recv_sem=ag_recv.at[at],
                device_id=(mz, partner), device_id_type=MESH,
            )
        )
        sends[-1].start()
        sends[-1].wait_recv()
        summed = summed + parts[at, 1]

    def quarter(index):
        return pl.ds(pl.multiple_of(index * share, 8), share)

    full[quarter(mz), :] = 0.25 * summed

    sends_z, receives_z = [], []
    for o in range(1, nz):
        peer, source = lax.rem(mz + o, nz), lax.rem(mz + nz - o, nz)
        for dst, to in ((mz, sends_z), (source, receives_z)):
            to.append(
                pltpu.make_async_remote_copy(
                    src_ref=full.at[quarter(mz)], dst_ref=full.at[quarter(dst)],
                    send_sem=fin_send.at[o], recv_sem=fin_recv.at[dst],
                    device_id=(peer, mx), device_id_type=MESH,
                )
            )
    for copy in sends_z:
        copy.start()
    for copy in receives_z:
        copy.wait_recv()
    for at, (out, first, count) in enumerate(
        ((g_mid, 0, hid), (g_in, hid, 2 * NF), (g_out, hid + 16, NF))
    ):
        stores.append(
            pltpu.make_async_copy(full.at[first : first + count], out, store_sem.at[4 + at])
        )
        stores[-1].start()
    for copy in stores:
        copy.wait()
    for k in range(3):
        for half in range(2):
            for copy in halo(k, half) + rims(k, half):
                copy.wait_send()
        for copy in level_copies(tg, 0, k)[0] + level_copies(tl, 1, k)[0]:
            copy.wait_send()
    for copy in scatter + sends + sends_z:
        copy.wait_send()


def write_out(*refs):
    sources, outs, held, sems = refs[:5], refs[5:10], refs[10:15], refs[15]
    loads = [pltpu.make_async_copy(sources[at], held[at], sems.at[0, at]) for at in range(5)]
    stores = [pltpu.make_async_copy(held[at], outs[at], sems.at[1, at]) for at in range(5)]
    for copy in loads:
        copy.start()
    for load, store in zip(loads, stores):
        load.wait()
        store.start()
    for copy in stores:
        copy.wait()


def on_device(nz, nx, state, state_cot, w_in, w_mid, w_out, radiation, fall_rate, active):
    fields, levels, columns = state.shape
    hid = w_in.shape[0]
    assert fields == NF and columns == 2 * LANES and hid == LANES and levels == 16
    assert nx & (nx - 1) == 0
    share = -(-(hid + 24) // (8 * nz)) * 8
    cells = levels * hid
    wide = NF * HALF
    chunk = (4, NF, levels, LANES)
    two = (2, NF, levels, LANES)
    dma = pltpu.SemaphoreType.DMA
    vmem = pltpu.VMEM
    scratch = [
        vmem(state.shape, F32),
        vmem(state.shape, F32),
        vmem((2 * NF, hid), BF16),
        vmem((hid, hid), BF16),
        vmem((NF, hid), BF16),
        vmem(radiation.shape, F32),
        vmem((1, columns), F32),
        vmem((1, columns), active.dtype),
        vmem((4,) + chunk, F32),
        vmem((4,) + two, F32),
        vmem(two, F32),
        vmem((3,) + two, F32),
        vmem((3,) + two, F32),
        vmem((2, 1, levels, LANES), F32),
        vmem((3, nz, levels + 8, columns), F32),
        vmem((3, nz, levels + 8, columns), F32),
        vmem((3,) + two, F32),
        vmem((3,) + two, F32),
        vmem((2, NF, HALF, LANES), F32),
        vmem((3, 2, 2 * wide, columns), BF16),
        vmem((2, wide, columns), BF16),
        vmem((3, cells, columns), F32),
        vmem((3, cells, columns), F32),
        vmem((3, cells, columns), BF16),
        vmem((3, cells, columns), BF16),
        vmem((cells // 2, 2 * wide), BF16),
        vmem((2 * wide, cells // 2), BF16),
        vmem((wide, cells // 2), BF16),
        vmem((cells // 2, wide), BF16),
        vmem((hid, hid), BF16),
        vmem((cells, columns), BF16),
        vmem((cells, columns), BF16),
        vmem(radiation.shape, F32),
        vmem((9, levels, columns), F32),
        vmem(two, F32),
        vmem(two, F32),
        vmem((hid, 2 * wide), F32),
        vmem((hid, wide), F32),
        vmem((hid, hid), F32),
        vmem((nz, share, LANES), F32),
        vmem((nz, share, LANES), F32),
        vmem((nx.bit_length() - 1, 2, share, LANES), F32),
        vmem((nz * share, LANES), F32),
        dma((8,)), dma((7,)),
        dma((2, 3, 2, 2)), dma((2, 3, 2, 2)),
        dma((2, 3, nz)), dma((2, 3, nz)),
        dma((nz,)), dma((nz,)),
        dma((nx,)), dma((nx,)),
        dma((nz,)), dma((nz,)),
    ]
    results = pl.pallas_call(
        functools.partial(kernel, nz, nx, levels, hid, share),
        out_shape=(
            jax.ShapeDtypeStruct(state.shape, F32),
            jax.ShapeDtypeStruct(state.shape, F32),
            jax.ShapeDtypeStruct((hid, hid), F32),
            jax.ShapeDtypeStruct((2 * NF, hid), F32),
            jax.ShapeDtypeStruct((NF, hid), F32),
        ),
        in_specs=[pl.BlockSpec(memory_space=pl.ANY)] * 8,
        out_specs=[pl.BlockSpec(memory_space=pl.ANY)] * 5,
        scratch_shapes=scratch,
        compiler_params=pltpu.CompilerParams(
            collective_id=0, has_side_effects=True, vmem_limit_bytes=56 * 1024 * 1024
        ),
        name="adjoint_step",
    )(
        state, state_cot, w_in.T, w_mid, w_out, radiation,
        fall_rate.reshape(1, columns), active.reshape(1, columns),
    )
    new_state, state_grad, g_mid, g_in, g_out = pl.pallas_call(
        write_out,
        out_shape=tuple(jax.ShapeDtypeStruct(r.shape, r.dtype) for r in results),
        in_specs=[pl.BlockSpec(memory_space=pl.ANY)] * 5,
        out_specs=[pl.BlockSpec(memory_space=pl.ANY)] * 5,
        scratch_shapes=[vmem(r.shape, r.dtype) for r in results] + [dma((2, 5))],
        compiler_params=pltpu.CompilerParams(vmem_limit_bytes=56 * 1024 * 1024),
        name="write_out",
    )(*results)
    return new_state, state_grad, g_in.T, g_mid, g_out


def solution(mesh):
    placed = (P(None, "gz", "gx"), P(None, "gz", "gx"), P(), P(), P(), P(), P("gx"), P("gx"))
    return jax.shard_map(
        functools.partial(on_device, mesh.shape["gz"], mesh.shape["gx"]),
        mesh=mesh,
        in_specs=placed,
        out_specs=(P(None, "gz", "gx"), P(None, "gz", "gx"), P(), P(), P()),
        check_vma=False,
    )
```

```python
import functools

import jax
import jax.numpy as jnp
from jax import lax
from jax.experimental import pallas as pl
from jax.experimental.pallas import tpu as pltpu
from jax.sharding import PartitionSpec as P

NF = 6
NY = 64
LANES = 128
HALF = 8
HALF_BITS = 3
MESH = pl.DeviceIdType.MESH
F32 = jnp.float32
BF16 = jnp.bfloat16


def mm(a, b, precision=None):
    return lax.dot_general(
        a, b, (((1,), (0,)), ((), ())), precision=precision, preferred_element_type=F32
    )


def mm_t(a, b, precision=None):
    return lax.dot_general(
        a, b, (((1,), (1,)), ((), ())), precision=precision, preferred_element_type=F32
    )


def iota(shape, dim):
    return lax.broadcasted_iota(jnp.int32, shape, dim)


def kernel(
    nz, nx, levels, hid, share,
    state_hbm, cot_hbm, w_in_hbm, w_mid_hbm, w_out_hbm, rad_hbm, fall_hbm, act_hbm,
    new_state, state_grad, g_mid, g_in, g_out,
    state, cot, w_in, w_mid, w_out, rad, fall, act, pick_in, pick_out,
    sp, lp, gp, rim_out, rim_in, fallv, tg, tl, dxs, dys, moved, feats, out_cot, t1s, t2s, h1s, h2s,
    k1, k1t, k2, k2t, wmt, pre1, pre2, by_in, by_out, radt, tab, fcs, acc, a_in, a_out, a_mid,
    pack, part, parts, full,
    load_sem, store_sem, halo_send, halo_recv, gz_send, gz_recv, rs_send, rs_recv, ag_send, ag_recv, fin_send, fin_recv,
):
    mz, mx = lax.axis_index("gz"), lax.axis_index("gx")
    left, right = lax.rem(mx + nx - 1, nx), lax.rem(mx + 1, nx)

    barrier = pltpu.get_barrier_semaphore()
    for o in range(1, nz):
        pl.semaphore_signal(
            barrier, inc=1, device_id=(lax.rem(mz + o, nz), mx), device_id_type=MESH
        )
    for o in range(1, nx):
        pl.semaphore_signal(
            barrier, inc=1, device_id=(mz, lax.rem(mx + o, nx)), device_id_type=MESH
        )

    loads = [
        pltpu.make_async_copy(src, dst, load_sem.at[at])
        for at, (src, dst) in enumerate(
            [
                (state_hbm, state), (cot_hbm, cot), (w_in_hbm, w_in), (w_mid_hbm, w_mid),
                (w_out_hbm, w_out), (rad_hbm, rad), (fall_hbm, fall), (act_hbm, act),
            ]
        )
    ]
    for copy in loads:
        copy.start()
    a_in[...] = jnp.zeros_like(a_in)
    a_out[...] = jnp.zeros_like(a_out)
    a_mid[...] = jnp.zeros_like(a_mid)
    for copy in loads:
        copy.wait()

    columns = 2 * LANES
    shape = (levels, columns)
    rate = jnp.broadcast_to(fall[...], shape)
    r1 = rate / (1.0 + rate)
    r2 = r1 * r1
    r4 = r2 * r2
    r8 = r4 * r4
    powers = [r1, r2, r4, r8, r8 * r8]
    up, down = jnp.ones(shape, F32), jnp.ones(shape, F32)
    level = iota(shape, 0)
    for bit in range(5):
        up = jnp.where(((level + 1) >> bit) & 1 == 1, up * powers[bit], up)
        down = jnp.where(((levels - level) >> bit) & 1 == 1, down * powers[bit], down)
    for at, value in enumerate(
        powers + [1.0 / (1.0 + rate), jnp.broadcast_to(act[...].astype(F32), shape), down, up]
    ):
        tab[at] = value

    for c in range(2):
        lanes = slice(c * LANES, (c + 1) * LANES)
        sp[0, c + 1] = state[:, :, lanes]
        lp[0, c] = (2.0 / 3.0) * cot[:, :, lanes]
        acc[c] = cot[:, :, lanes] * (1.0 / 3.0)

    def rows_of(half):
        return pl.ds(pl.multiple_of(half * HALF, HALF), HALF)

    def sides(sources, targets, kind, k, half):
        return [
            pltpu.make_async_remote_copy(
                src_ref=sources[side].at[:, rows_of(half), :],
                dst_ref=targets[side].at[:, rows_of(half), :],
                send_sem=halo_send.at[kind, k, half, side],
                recv_sem=halo_recv.at[kind, k, half, side],
                device_id=(mz, (left, right)[side]), device_id_type=MESH,
            )
            for side in range(2)
        ]

    def halo(k, half):
        return sides((sp.at[k, 1], sp.at[k, 2]), (sp.at[k, 3], sp.at[k, 0]), 0, k, half)

    def rims(i, half):
        return sides((rim_out.at[i, 0], rim_out.at[i, 1]), (rim_in.at[i, 1], rim_in.at[i, 0]), 1, i, half)

    pl.semaphore_wait(barrier, nz - 1 + nx - 1)
    for half in range(2):
        for copy in halo(0, half):
            copy.start()

    def level_copies(buf, kind, k):
        sends, receives = [], []
        for o in range(1, nz):
            peer, source = lax.rem(mz + o, nz), lax.rem(mz + nz - o, nz)
            for dst, to in ((mz, sends), (source, receives)):
                to.append(
                    pltpu.make_async_remote_copy(
                        src_ref=buf.at[k, mz], dst_ref=buf.at[k, dst],
                        send_sem=gz_send.at[kind, k, o], recv_sem=gz_recv.at[kind, k, dst],
                        device_id=(peer, mx), device_id_type=MESH,
                    )
                )
        return sends, receives

    lane = iota((1, 1, LANES), 2)
    low = lane < NY
    y_last, y_first = lane & (NY - 1) == NY - 1, lane & (NY - 1) == 0
    depth = iota((levels, LANES), 0)

    def along_x(chunks):
        turned = [pltpu.roll(chunk, NY, 2) for chunk in chunks]
        out = []
        for i in (1, 2):
            plus = jnp.where(low, turned[i], turned[i + 1])
            minus = jnp.where(low, turned[i - 1], turned[i])
            out.append((plus, minus, (8.0 * (plus - minus) - (chunks[i + 1] - chunks[i - 1])) * (1.0 / 12.0)))
        return out

    def along_y(chunk):
        plus = jnp.where(y_last, pltpu.roll(chunk, NY - 1, 2), pltpu.roll(chunk, LANES - 1, 2))
        minus = jnp.where(y_first, pltpu.roll(chunk, NY + 1, 2), pltpu.roll(chunk, 1, 2))
        return plus, minus

    def settle(source, lanes, downward):
        value = tab[5, :, lanes] * source
        for bit in range(4):
            step = 1 << bit
            if downward:
                moved_by = pltpu.roll(value, levels - step, 0)
                inside = depth < levels - step
            else:
                moved_by = pltpu.roll(value, step, 0)
                inside = depth >= step
            value = value + tab[bit, :, lanes] * jnp.where(inside, moved_by, 0.0)
        return value

    def inflow(buf, k, lanes, downward):
        total = jnp.zeros((8, LANES), F32)
        order = range(nz - 1, 0, -1) if downward else range(nz - 1)
        for j in order:
            reached = j > mz if downward else j < mz
            following = buf[k, j, levels:, lanes] + tab[4, 0:8, lanes] * total
            total = jnp.where(reached, following, total)
        return total[0:1]

    def chunk_lanes(c):
        return slice(c * LANES, (c + 1) * LANES)

    def share_levels(k):
        for c in range(2):
            lanes = chunk_lanes(c)
            value = settle(sp[k, c + 1, 5], lanes, True)
            fallv[c, 0] = value
            tg[k, mz, 0:levels, lanes] = sp[k, c + 1, 3]
            tg[k, mz, levels:, lanes] = jnp.broadcast_to(value[0:1], (8, LANES))
        for copy in level_copies(tg, 0, k)[0]:
            copy.start()

    share_levels(0)

    def spread_t(rows, cols):
        return (iota((rows, cols), 0) >> HALF_BITS == iota((rows, cols), 1)).astype(F32).astype(BF16)

    eye = (iota((hid, hid), 0) == iota((hid, hid), 1)).astype(F32).astype(BF16)
    w1t = mm(spread_t(2 * NF * HALF, 2 * NF), w_in[...])
    w1 = mm_t(eye, w1t.astype(BF16))
    w2 = mm(spread_t(NF * HALF, NF), w_out[...])
    w2t = mm_t(eye, w2.astype(BF16))
    wmt[...] = mm_t(eye, w_mid[...]).astype(BF16)

    def place(z, carry):
        rows = pl.ds(pl.multiple_of(z * hid, hid), hid)
        k1[rows, :] = jnp.where(iota(w1.shape, 1) & (HALF - 1) == z, w1, 0.0).astype(BF16)
        k2t[rows, :] = jnp.where(iota(w2t.shape, 1) & (HALF - 1) == z, w2t, 0.0).astype(BF16)
        k1t[:, rows] = jnp.where(iota(w1t.shape, 0) & (HALF - 1) == z, w1t, 0.0).astype(BF16)
        k2[:, rows] = jnp.where(iota(w2.shape, 0) & (HALF - 1) == z, w2, 0.0).astype(BF16)
        return carry

    lax.fori_loop(0, HALF, place, 0)
    radt[...] = rad[...].T

    def gathered(cols):
        at = iota((HALF * 16, cols), 0)
        return ((at & 15) * HALF + (at >> 4) == iota((HALF * 16, cols), 1)).astype(F32).astype(BF16)

    pick_in[...] = gathered(2 * NF * HALF)
    pick_out[...] = gathered(NF * HALF)


    def forward(t, carry):
        k, half = t >> 1, t & 1
        rows8 = rows_of(half)
        own = [sp[k, 1, :, rows8, :], sp[k, 2, :, rows8, :]]
        for copy in halo(k, half):
            copy.wait_recv()
        x_sides = along_x([sp[k, 0, :, rows8, :], own[0], own[1], sp[k, 3, :, rows8, :]])
        for c in range(2):
            y_plus, y_minus = along_y(own[c])
            x_plus, x_minus, deriv_x = x_sides[c]
            deriv_y = (y_plus - y_minus) * 0.5
            laplace = x_plus + x_minus + y_plus + y_minus - 4.0 * own[c]
            dxs[k, c, :, rows8, :] = deriv_x
            dys[k, c, :, rows8, :] = deriv_y
            moved[c] = -(own[c][0:1] * deriv_x + own[c][1:2] * deriv_y) + 0.1 * laplace
            feats[k, half, 0 : NF * HALF, chunk_lanes(c)] = (
                own[c].reshape(NF * HALF, LANES).astype(BF16)
            )
            feats[k, half, NF * HALF :, chunk_lanes(c)] = (
                deriv_x.reshape(NF * HALF, LANES).astype(BF16)
            )

        def layers(group, inner):
            block = pl.ds(pl.multiple_of(group * (4 * hid), 4 * hid), 4 * hid)
            first = half * (HALF * hid) + group * (4 * hid)
            kept = pl.ds(pl.multiple_of(first, 4 * hid), 4 * hid)
            middle = w_mid[...]
            t1 = jnp.tanh(mm(k1[block, :], feats[k, half]))
            h1 = t1.astype(BF16)
            t2 = [jnp.tanh(mm(middle, h1[j * hid : (j + 1) * hid])) for j in range(4)]
            t1s[k, kept, :] = t1
            h1s[k, kept, :] = h1
            for j in range(4):
                rows = pl.ds(pl.multiple_of(first + j * hid, hid), hid)
                t2s[k, rows, :] = t2[j]
                h2s[k, rows, :] = t2[j].astype(BF16)
            return inner

        lax.fori_loop(0, HALF // 4, layers, 0)
        half_cells = pl.ds(pl.multiple_of(half * (HALF * hid), HALF * hid), HALF * hid)
        closure = mm(k2[...], h2s[k, half_cells, :])

        @pl.when(half == 0)
        def _():
            for copy in level_copies(tg, 0, k)[1]:
                copy.wait_recv()

        heat = mm(
            rad[pl.ds(pl.multiple_of(mz * levels + half * HALF, HALF), HALF), :],
            tg[k, :, 0:levels, :].reshape(nz * levels, columns),
            lax.Precision.HIGHEST,
        )
        keep = jnp.where(k == 0, 0.0, jnp.where(k == 1, 0.75, 1.0 / 3.0))
        take = jnp.where(k == 0, 1.0, jnp.where(k == 1, 0.25, 2.0 / 3.0))
        for c in range(2):
            lanes = chunk_lanes(c)
            total = moved[c] + closure[:, lanes].reshape(NF, HALF, LANES)
            fallen = fallv[c, 0, rows8, :] + tab[7, rows8, lanes] * inflow(tg, k, lanes, True)
            total = jnp.concatenate(
                [
                    total[0:3],
                    total[3:4] + heat[:, lanes][None],
                    total[4:5],
                    total[5:6] + (tab[6, rows8, lanes] * (fallen - own[c][5]))[None],
                ],
                0,
            )
            sp[k + 1, c + 1, :, rows8, :] = (
                keep * state[:, rows8, lanes] + take * (own[c] + 0.25 * total)
            )

        @pl.when(k < 2)
        def _():
            for copy in halo(k + 1, half):
                copy.start()

            @pl.when(half == 1)
            def _():
                share_levels(k + 1)

        return carry

    lax.fori_loop(0, 6, forward, 0)
    stores = []
    for c in range(2):
        stores.append(
            pltpu.make_async_copy(
                sp.at[3, c + 1], new_state.at[:, :, chunk_lanes(c)], store_sem.at[c]
            )
        )
        stores[-1].start()


    total_rows = nz * share
    scatter = []
    for o in range(1, nz):
        peer = lax.rem(mz + o, nz)
        scatter.append(
            pltpu.make_async_remote_copy(
                src_ref=pack.at[peer], dst_ref=part.at[o],
                send_sem=rs_send.at[o], recv_sem=rs_recv.at[o],
                device_id=(peer, mx), device_id_type=MESH,
            )
        )

    def backward(i, carry):
        k = 2 - i
        lam = [lp[i, 0], lp[i, 1]]
        local, masked = [], []
        for c in range(2):
            lanes = chunk_lanes(c)
            source = tab[6, :, lanes] * lam[c][5]
            value = settle(source, lanes, False)
            masked.append(source)
            local.append(value)
            tl[i, mz, 0:levels, lanes] = lam[c][3]
            tl[i, mz, levels:, lanes] = jnp.broadcast_to(value[levels - 1 : levels], (8, LANES))
            for half in range(2):
                out_cot[half, :, lanes] = (
                    lam[c][:, half * HALF : (half + 1) * HALF, :]
                    .reshape(NF * HALF, LANES).astype(BF16)
                )
        sends, receives = level_copies(tl, 1, i)
        for copy in sends:
            copy.start()

        def by_half(half, outer):
            rows8 = rows_of(half)

            def layers(group, inner):
                block = pl.ds(pl.multiple_of(group * (4 * hid), 4 * hid), 4 * hid)
                first = half * (HALF * hid) + group * (4 * hid)
                kept = pl.ds(pl.multiple_of(first, 4 * hid), 4 * hid)
                t2 = t2s[k, kept, :]
                t1 = t1s[k, kept, :]
                middle = wmt[...]
                p2 = (mm(k2t[block, :], out_cot[half]) * (1.0 - t2 * t2)).astype(BF16)
                p1 = []
                for j in range(4):
                    part_rows = slice(j * hid, (j + 1) * hid)
                    back = mm(middle, p2[part_rows])
                    p1.append((back * (1.0 - t1[part_rows] * t1[part_rows])).astype(BF16))
                pre2[kept, :] = p2
                for j in range(4):
                    rows = pl.ds(pl.multiple_of(first + j * hid, hid), hid)
                    pre1[rows, :] = p1[j]
                return inner

            lax.fori_loop(0, HALF // 4, layers, 0)
            half_cells = pl.ds(pl.multiple_of(half * (HALF * hid), HALF * hid), HALF * hid)
            feature_cot = mm(k1t[...], pre1[half_cells, :])
            for c in range(2):
                lanes = chunk_lanes(c)
                fcs[c, :, rows8, :] = feature_cot[0 : NF * HALF, lanes].reshape(NF, HALF, LANES)
                now = lp[i, c, :, rows8, :]
                source = (
                    feature_cot[NF * HALF :, lanes].reshape(NF, HALF, LANES)
                    - sp[k, c + 1, 0:1, rows8, :] * now
                )
                gp[c, :, rows8, :] = source
                turned = pltpu.roll(source, NY, 2)
                spread_lam = 0.1 * pltpu.roll(now, NY, 2)
                if c == 0:
                    near = (source - 8.0 * turned) * (1.0 / 12.0) + spread_lam
                    rim_out[i, 0, :, rows8, :] = jnp.where(low, source * (1.0 / 12.0), near)
                else:
                    near = (8.0 * turned - source) * (1.0 / 12.0) + spread_lam
                    rim_out[i, 1, :, rows8, :] = jnp.where(low, near, source * (-1.0 / 12.0))
            for copy in rims(i, half):
                copy.start()
            few = pl.ds(pl.multiple_of(half * (HALF * 16), HALF * 16), HALF * 16)
            by_in[few, :] = mm(pick_in[...], feats[k, half]).astype(BF16)
            by_out[few, :] = mm(pick_out[...], out_cot[half]).astype(BF16)
            return outer

        lax.fori_loop(0, 2, by_half, 0)

        def terms(group, inner):
            s_in, s_out, s_mid = inner
            for j in range(4):
                z = group * 4 + j
                rows = pl.ds(pl.multiple_of(z * hid, hid), hid)
                few = pl.ds(pl.multiple_of(z * 16, 16), 16)
                s_mid = s_mid + mm_t(pre2[rows, :], h1s[k, rows, :])
                s_in = s_in + mm_t(by_in[few, :], pre1[rows, :])
                s_out = s_out + mm_t(by_out[few, :], h2s[k, rows, :])
            return s_in, s_out, s_mid

        s_in, s_out, s_mid = lax.fori_loop(
            0, levels // 4, terms, (a_in[...], a_out[...], a_mid[...])
        )
        a_in[...] = s_in
        a_out[...] = s_out
        a_mid[...] = s_mid

        @pl.when(k == 0)
        def _():
            everything = jnp.concatenate(
                [
                    a_mid[...],
                    a_in[...],
                    a_out[0:8, :],
                    jnp.zeros((total_rows - hid - 24, LANES), F32),
                ],
                0,
            )
            pack[...] = everything.reshape(nz, share, LANES)
            for copy in scatter:
                copy.start()

        for copy in receives:
            copy.wait_recv()
        heat = mm(
            radt[pl.ds(pl.multiple_of(mz * levels, levels), levels), :],
            tl[i, :, 0:levels, :].reshape(nz * levels, columns),
            lax.Precision.HIGHEST,
        )
        zero = jnp.zeros((NF, levels, LANES), F32)
        lam_sides = along_x([zero, lam[0], lam[1], zero])
        g_sides = along_x([zero, gp[0], gp[1], zero])
        for half in range(2):
            for copy in rims(i, half):
                copy.wait_recv()
        weight = jnp.where(k == 0, 1.0, jnp.where(k == 1, 0.0, 0.75))
        share_on = jnp.where(k == 2, 0.25, 1.0)
        for c in range(2):
            lanes = chunk_lanes(c)
            now = lam[c]
            y_plus, y_minus = along_y(now)
            x_plus, x_minus, _ = lam_sides[c]
            carried_plus, carried_minus = along_y(sp[k, c + 1, 1:2] * now)
            back = (
                (carried_plus - carried_minus) * 0.5
                - g_sides[c][2]
                + 0.1 * (x_plus + x_minus + y_plus + y_minus - 4.0 * now)
                + fcs[c]
                + rim_in[i, c]
            )
            pulled = local[c] + tab[8, :, lanes] * inflow(tl, i, lanes, False)
            back = jnp.concatenate(
                [
                    back[0:1] - jnp.sum(now * dxs[k, c], axis=0, keepdims=True),
                    back[1:2] - jnp.sum(now * dys[k, c], axis=0, keepdims=True),
                    back[2:3],
                    back[3:4] + heat[:, lanes][None],
                    back[4:5],
                    back[5:6] + (pulled - masked[c])[None],
                ],
                0,
            )
            whole = now + 0.25 * back
            acc[c] = acc[c] + weight * whole
            lp[i + 1, c] = share_on * whole
        return carry

    lax.fori_loop(0, 3, backward, 0)
    for c in range(2):
        stores.append(
            pltpu.make_async_copy(
                acc.at[c], state_grad.at[:, :, chunk_lanes(c)], store_sem.at[2 + c]
            )
        )
        stores[-1].start()

    mine = pack[mz]
    for o in range(1, nz):
        scatter[o - 1].wait_recv()
        mine = mine + part[o]
    parts[mx] = mine

    sends, receives = [], []
    for o in range(1, nx):
        peer, source = lax.rem(mx + o, nx), lax.rem(mx + nx - o, nx)
        for dst, to in ((mx, sends), (source, receives)):
            to.append(
                pltpu.make_async_remote_copy(
                    src_ref=parts.at[mx], dst_ref=parts.at[dst],
                    send_sem=ag_send.at[o], recv_sem=ag_recv.at[dst],
                    device_id=(mz, peer), device_id_type=MESH,
                )
            )
    for copy in sends:
        copy.start()
    for copy in receives:
        copy.wait_recv()
    summed = parts[0]
    for j in range(1, nx):
        summed = summed + parts[j]

    def quarter(index):
        return pl.ds(pl.multiple_of(index * share, 8), share)

    full[quarter(mz), :] = 0.25 * summed

    sends_z, receives_z = [], []
    for o in range(1, nz):
        peer, source = lax.rem(mz + o, nz), lax.rem(mz + nz - o, nz)
        for dst, to in ((mz, sends_z), (source, receives_z)):
            to.append(
                pltpu.make_async_remote_copy(
                    src_ref=full.at[quarter(mz)], dst_ref=full.at[quarter(dst)],
                    send_sem=fin_send.at[o], recv_sem=fin_recv.at[dst],
                    device_id=(peer, mx), device_id_type=MESH,
                )
            )
    for copy in sends_z:
        copy.start()
    for copy in receives_z:
        copy.wait_recv()
    for at, (out, first, count) in enumerate(
        ((g_mid, 0, hid), (g_in, hid, 2 * NF), (g_out, hid + 16, NF))
    ):
        stores.append(
            pltpu.make_async_copy(full.at[first : first + count], out, store_sem.at[4 + at])
        )
        stores[-1].start()
    for copy in stores:
        copy.wait()
    for k in range(3):
        for half in range(2):
            for copy in halo(k, half) + rims(k, half):
                copy.wait_send()
        for copy in level_copies(tg, 0, k)[0] + level_copies(tl, 1, k)[0]:
            copy.wait_send()
    for copy in scatter + sends + sends_z:
        copy.wait_send()


def write_out(*refs):
    sources, outs, held, sems = refs[:5], refs[5:10], refs[10:15], refs[15]
    loads = [pltpu.make_async_copy(sources[at], held[at], sems.at[0, at]) for at in range(5)]
    stores = [pltpu.make_async_copy(held[at], outs[at], sems.at[1, at]) for at in range(5)]
    for copy in loads:
        copy.start()
    for load, store in zip(loads, stores):
        load.wait()
        store.start()
    for copy in stores:
        copy.wait()


def on_device(nz, nx, state, state_cot, w_in, w_mid, w_out, radiation, fall_rate, active):
    fields, levels, columns = state.shape
    hid = w_in.shape[0]
    assert fields == NF and columns == 2 * LANES and hid == LANES and levels == 16
    share = -(-(hid + 24) // (8 * nz)) * 8
    cells = levels * hid
    wide = NF * HALF
    chunk = (4, NF, levels, LANES)
    two = (2, NF, levels, LANES)
    dma = pltpu.SemaphoreType.DMA
    vmem = pltpu.VMEM
    scratch = [
        vmem(state.shape, F32),
        vmem(state.shape, F32),
        vmem((2 * NF, hid), BF16),
        vmem((hid, hid), BF16),
        vmem((NF, hid), BF16),
        vmem(radiation.shape, F32),
        vmem((1, columns), F32),
        vmem((1, columns), active.dtype),
        vmem((HALF * 16, 2 * wide), BF16),
        vmem((HALF * 16, wide), BF16),
        vmem((4,) + chunk, F32),
        vmem((4,) + two, F32),
        vmem(two, F32),
        vmem((3,) + two, F32),
        vmem((3,) + two, F32),
        vmem((2, 1, levels, LANES), F32),
        vmem((3, nz, levels + 8, columns), F32),
        vmem((3, nz, levels + 8, columns), F32),
        vmem((3,) + two, F32),
        vmem((3,) + two, F32),
        vmem((2, NF, HALF, LANES), F32),
        vmem((3, 2, 2 * wide, columns), BF16),
        vmem((2, wide, columns), BF16),
        vmem((3, cells, columns), F32),
        vmem((3, cells, columns), F32),
        vmem((3, cells, columns), BF16),
        vmem((3, cells, columns), BF16),
        vmem((cells // 2, 2 * wide), BF16),
        vmem((2 * wide, cells // 2), BF16),
        vmem((wide, cells // 2), BF16),
        vmem((cells // 2, wide), BF16),
        vmem((hid, hid), BF16),
        vmem((cells, columns), BF16),
        vmem((cells, columns), BF16),
        vmem((levels * 16, columns), BF16),
        vmem((levels * 16, columns), BF16),
        vmem(radiation.shape, F32),
        vmem((9, levels, columns), F32),
        vmem(two, F32),
        vmem(two, F32),
        vmem((16, hid), F32),
        vmem((16, hid), F32),
        vmem((hid, hid), F32),
        vmem((nz, share, LANES), F32),
        vmem((nz, share, LANES), F32),
        vmem((nx, share, LANES), F32),
        vmem((nz * share, LANES), F32),
        dma((8,)), dma((7,)),
        dma((2, 3, 2, 2)), dma((2, 3, 2, 2)),
        dma((2, 3, nz)), dma((2, 3, nz)),
        dma((nz,)), dma((nz,)),
        dma((nx,)), dma((nx,)),
        dma((nz,)), dma((nz,)),
    ]
    results = pl.pallas_call(
        functools.partial(kernel, nz, nx, levels, hid, share),
        out_shape=(
            jax.ShapeDtypeStruct(state.shape, F32),
            jax.ShapeDtypeStruct(state.shape, F32),
            jax.ShapeDtypeStruct((hid, hid), F32),
            jax.ShapeDtypeStruct((2 * NF, hid), F32),
            jax.ShapeDtypeStruct((NF, hid), F32),
        ),
        in_specs=[pl.BlockSpec(memory_space=pl.ANY)] * 8,
        out_specs=[pl.BlockSpec(memory_space=pl.ANY)] * 5,
        scratch_shapes=scratch,
        compiler_params=pltpu.CompilerParams(
            collective_id=0, has_side_effects=True, vmem_limit_bytes=56 * 1024 * 1024
        ),
        name="adjoint_step",
    )(
        state, state_cot, w_in.T, w_mid, w_out, radiation,
        fall_rate.reshape(1, columns), active.reshape(1, columns),
    )
    new_state, state_grad, g_mid, g_in, g_out = pl.pallas_call(
        write_out,
        out_shape=tuple(jax.ShapeDtypeStruct(r.shape, r.dtype) for r in results),
        in_specs=[pl.BlockSpec(memory_space=pl.ANY)] * 5,
        out_specs=[pl.BlockSpec(memory_space=pl.ANY)] * 5,
        scratch_shapes=[vmem(r.shape, r.dtype) for r in results] + [dma((2, 5))],
        compiler_params=pltpu.CompilerParams(vmem_limit_bytes=56 * 1024 * 1024),
        name="write_out",
    )(*results)
    return new_state, state_grad, g_in.T, g_mid, g_out


def solution(mesh):
    placed = (P(None, "gz", "gx"), P(None, "gz", "gx"), P(), P(), P(), P(), P("gx"), P("gx"))
    return jax.shard_map(
        functools.partial(on_device, mesh.shape["gz"], mesh.shape["gx"]),
        mesh=mesh,
        in_specs=placed,
        out_specs=(P(None, "gz", "gx"), P(None, "gz", "gx"), P(), P(), P()),
        check_vma=False,
    )
```

```python
import functools

import jax
import jax.numpy as jnp
from jax import lax
from jax.experimental import pallas as pl
from jax.experimental.pallas import tpu as pltpu
from jax.sharding import PartitionSpec as P

NF = 6
NY = 64
LANES = 128
HALF = 8
HALF_BITS = 3
MESH = pl.DeviceIdType.MESH
F32 = jnp.float32
BF16 = jnp.bfloat16


def mm(a, b, precision=None):
    return lax.dot_general(
        a, b, (((1,), (0,)), ((), ())), precision=precision, preferred_element_type=F32
    )


def mm_t(a, b, precision=None):
    return lax.dot_general(
        a, b, (((1,), (1,)), ((), ())), precision=precision, preferred_element_type=F32
    )


def iota(shape, dim):
    return lax.broadcasted_iota(jnp.int32, shape, dim)


def kernel(
    nz, nx, levels, hid, share,
    state_hbm, cot_hbm, w_in_hbm, w_mid_hbm, w_out_hbm, rad_hbm, fall_hbm, act_hbm,
    new_state, state_grad, g_mid, g_in, g_out,
    state, cot, w_in, w_mid, w_out, rad, fall, act, pick_in, pick_out,
    sp, lp, gp, rim_out, rim_in, fallv, heats, tg, tl, dxs, dys, moved, feats, out_cot, t1s, t2s, h1s, h2s,
    k1, k1t, k2, k2t, wmt, pre1, pre2, by_in, by_out, radt, tab, fcs, acc, a_in, a_out, a_mid,
    pack, part, parts, full,
    load_sem, store_sem, halo_send, halo_recv, gz_send, gz_recv, rs_send, rs_recv, ag_send, ag_recv, fin_send, fin_recv,
):
    mz, mx = lax.axis_index("gz"), lax.axis_index("gx")
    left, right = lax.rem(mx + nx - 1, nx), lax.rem(mx + 1, nx)

    barrier = pltpu.get_barrier_semaphore()
    for o in range(1, nz):
        pl.semaphore_signal(
            barrier, inc=1, device_id=(lax.rem(mz + o, nz), mx), device_id_type=MESH
        )
    for o in range(1, nx):
        pl.semaphore_signal(
            barrier, inc=1, device_id=(mz, lax.rem(mx + o, nx)), device_id_type=MESH
        )

    loads = [
        pltpu.make_async_copy(src, dst, load_sem.at[at])
        for at, (src, dst) in enumerate(
            [
                (state_hbm, state), (cot_hbm, cot), (w_in_hbm, w_in), (w_mid_hbm, w_mid),
                (w_out_hbm, w_out), (rad_hbm, rad), (fall_hbm, fall), (act_hbm, act),
            ]
        )
    ]
    for copy in loads:
        copy.start()
    a_in[...] = jnp.zeros_like(a_in)
    a_out[...] = jnp.zeros_like(a_out)
    a_mid[...] = jnp.zeros_like(a_mid)
    for copy in loads:
        copy.wait()

    columns = 2 * LANES
    shape = (levels, columns)
    rate = jnp.broadcast_to(fall[...], shape)
    r1 = rate / (1.0 + rate)
    r2 = r1 * r1
    r4 = r2 * r2
    r8 = r4 * r4
    powers = [r1, r2, r4, r8, r8 * r8]
    up, down = jnp.ones(shape, F32), jnp.ones(shape, F32)
    level = iota(shape, 0)
    for bit in range(5):
        up = jnp.where(((level + 1) >> bit) & 1 == 1, up * powers[bit], up)
        down = jnp.where(((levels - level) >> bit) & 1 == 1, down * powers[bit], down)
    for at, value in enumerate(
        powers + [1.0 / (1.0 + rate), jnp.broadcast_to(act[...].astype(F32), shape), down, up]
    ):
        tab[at] = value

    for c in range(2):
        lanes = slice(c * LANES, (c + 1) * LANES)
        sp[0, c + 1] = state[:, :, lanes]
        lp[0, c] = (2.0 / 3.0) * cot[:, :, lanes]
        acc[c] = cot[:, :, lanes] * (1.0 / 3.0)

    def rows_of(half):
        return pl.ds(pl.multiple_of(half * HALF, HALF), HALF)

    def sides(sources, targets, kind, k, half):
        return [
            pltpu.make_async_remote_copy(
                src_ref=sources[side].at[:, rows_of(half), :],
                dst_ref=targets[side].at[:, rows_of(half), :],
                send_sem=halo_send.at[kind, k, half, side],
                recv_sem=halo_recv.at[kind, k, half, side],
                device_id=(mz, (left, right)[side]), device_id_type=MESH,
            )
            for side in range(2)
        ]

    def halo(k, half):
        return sides((sp.at[k, 1], sp.at[k, 2]), (sp.at[k, 3], sp.at[k, 0]), 0, k, half)

    def rims(i, half):
        return sides((rim_out.at[i, 0], rim_out.at[i, 1]), (rim_in.at[i, 1], rim_in.at[i, 0]), 1, i, half)

    pl.semaphore_wait(barrier, nz - 1 + nx - 1)
    for half in range(2):
        for copy in halo(0, half):
            copy.start()

    def level_copies(buf, kind, k):
        sends, receives = [], []
        for o in range(1, nz):
            peer, source = lax.rem(mz + o, nz), lax.rem(mz + nz - o, nz)
            for dst, to in ((mz, sends), (source, receives)):
                to.append(
                    pltpu.make_async_remote_copy(
                        src_ref=buf.at[k, mz], dst_ref=buf.at[k, dst],
                        send_sem=gz_send.at[kind, k, o], recv_sem=gz_recv.at[kind, k, dst],
                        device_id=(peer, mx), device_id_type=MESH,
                    )
                )
        return sends, receives

    lane = iota((1, 1, LANES), 2)
    low = lane < NY
    y_last, y_first = lane & (NY - 1) == NY - 1, lane & (NY - 1) == 0
    depth = iota((levels, LANES), 0)

    def along_x(chunks):
        turned = [pltpu.roll(chunk, NY, 2) for chunk in chunks]
        out = []
        for i in (1, 2):
            plus = jnp.where(low, turned[i], turned[i + 1])
            minus = jnp.where(low, turned[i - 1], turned[i])
            out.append((plus, minus, (8.0 * (plus - minus) - (chunks[i + 1] - chunks[i - 1])) * (1.0 / 12.0)))
        return out

    def along_y(chunk):
        plus = jnp.where(y_last, pltpu.roll(chunk, NY - 1, 2), pltpu.roll(chunk, LANES - 1, 2))
        minus = jnp.where(y_first, pltpu.roll(chunk, NY + 1, 2), pltpu.roll(chunk, 1, 2))
        return plus, minus

    def settle(source, lanes, downward):
        value = tab[5, :, lanes] * source
        for bit in range(4):
            step = 1 << bit
            if downward:
                moved_by = pltpu.roll(value, levels - step, 0)
                inside = depth < levels - step
            else:
                moved_by = pltpu.roll(value, step, 0)
                inside = depth >= step
            value = value + tab[bit, :, lanes] * jnp.where(inside, moved_by, 0.0)
        return value

    def inflow(buf, k, lanes, downward):
        total = jnp.zeros((8, LANES), F32)
        order = range(nz - 1, 0, -1) if downward else range(nz - 1)
        for j in order:
            reached = j > mz if downward else j < mz
            following = buf[k, j, levels:, lanes] + tab[4, 0:8, lanes] * total
            total = jnp.where(reached, following, total)
        return total[0:1]

    def chunk_lanes(c):
        return slice(c * LANES, (c + 1) * LANES)

    def share_levels(k):
        for c in range(2):
            lanes = chunk_lanes(c)
            value = settle(sp[k, c + 1, 5], lanes, True)
            fallv[c, 0] = value
            tg[k, mz, 0:levels, lanes] = sp[k, c + 1, 3]
            tg[k, mz, levels:, lanes] = jnp.broadcast_to(value[0:1], (8, LANES))
        for copy in level_copies(tg, 0, k)[0]:
            copy.start()

    share_levels(0)

    def spread_t(rows, cols):
        return (iota((rows, cols), 0) >> HALF_BITS == iota((rows, cols), 1)).astype(F32).astype(BF16)

    eye = (iota((hid, hid), 0) == iota((hid, hid), 1)).astype(F32).astype(BF16)
    w1t = mm(spread_t(2 * NF * HALF, 2 * NF), w_in[...])
    w1 = mm_t(eye, w1t.astype(BF16))
    w2 = mm(spread_t(NF * HALF, NF), w_out[...])
    w2t = mm_t(eye, w2.astype(BF16))
    wmt[...] = mm_t(eye, w_mid[...]).astype(BF16)

    def place(z, carry):
        rows = pl.ds(pl.multiple_of(z * hid, hid), hid)
        k1[rows, :] = jnp.where(iota(w1.shape, 1) & (HALF - 1) == z, w1, 0.0).astype(BF16)
        k2t[rows, :] = jnp.where(iota(w2t.shape, 1) & (HALF - 1) == z, w2t, 0.0).astype(BF16)
        k1t[:, rows] = jnp.where(iota(w1t.shape, 0) & (HALF - 1) == z, w1t, 0.0).astype(BF16)
        k2[:, rows] = jnp.where(iota(w2.shape, 0) & (HALF - 1) == z, w2, 0.0).astype(BF16)
        return carry

    lax.fori_loop(0, HALF, place, 0)
    radt[...] = rad[...].T

    def gathered(cols):
        at = iota((HALF * 16, cols), 0)
        return ((at & 15) * HALF + (at >> 4) == iota((HALF * 16, cols), 1)).astype(F32).astype(BF16)

    pick_in[...] = gathered(2 * NF * HALF)
    pick_out[...] = gathered(NF * HALF)


    def forward(t, carry):
        k, half = t >> 1, t & 1
        rows8 = rows_of(half)
        own = [sp[k, 1, :, rows8, :], sp[k, 2, :, rows8, :]]
        y_sides = [along_y(chunk) for chunk in own]
        carried, spread_y = [], []
        for c in range(2):
            y_plus, y_minus = y_sides[c]
            deriv_y = (y_plus - y_minus) * 0.5
            dys[k, c, :, rows8, :] = deriv_y
            carried.append(own[c][1:2] * deriv_y)
            spread_y.append(y_plus + y_minus - 4.0 * own[c])
            feats[k, half, 0 : NF * HALF, chunk_lanes(c)] = (
                own[c].reshape(NF * HALF, LANES).astype(BF16)
            )
        for copy in halo(k, half):
            copy.wait_recv()
        x_sides = along_x([sp[k, 0, :, rows8, :], own[0], own[1], sp[k, 3, :, rows8, :]])
        for c in range(2):
            x_plus, x_minus, deriv_x = x_sides[c]
            dxs[k, c, :, rows8, :] = deriv_x
            moved[c] = -(own[c][0:1] * deriv_x + carried[c]) + 0.1 * (
                x_plus + x_minus + spread_y[c]
            )
            feats[k, half, NF * HALF :, chunk_lanes(c)] = (
                deriv_x.reshape(NF * HALF, LANES).astype(BF16)
            )

        def layers(group, inner):
            block = pl.ds(pl.multiple_of(group * (HALF * hid), HALF * hid), HALF * hid)
            first = half * (HALF * hid) + group * (HALF * hid)
            kept = pl.ds(pl.multiple_of(first, HALF * hid), HALF * hid)
            middle = w_mid[...]
            t1 = jnp.tanh(mm(k1[block, :], feats[k, half]))
            h1 = t1.astype(BF16)
            t2 = [jnp.tanh(mm(middle, h1[j * hid : (j + 1) * hid])) for j in range(HALF)]
            t1s[k, kept, :] = t1
            h1s[k, kept, :] = h1
            for j in range(HALF):
                rows = pl.ds(pl.multiple_of(first + j * hid, hid), hid)
                t2s[k, rows, :] = t2[j]
                h2s[k, rows, :] = t2[j].astype(BF16)
            return inner

        layers(0, 0)
        half_cells = pl.ds(pl.multiple_of(half * (HALF * hid), HALF * hid), HALF * hid)
        closure = mm(k2[...], h2s[k, half_cells, :])

        @pl.when(half == 0)
        def _():
            for copy in level_copies(tg, 0, k)[1]:
                copy.wait_recv()
            heats[...] = mm(
                rad[pl.ds(pl.multiple_of(mz * levels, levels), levels), :],
                tg[k, :, 0:levels, :].reshape(nz * levels, columns),
                lax.Precision.HIGHEST,
            )
            for c in range(2):
                lanes = chunk_lanes(c)
                fallv[c, 0] = fallv[c, 0] + tab[7, :, lanes] * inflow(tg, k, lanes, True)

        keep = jnp.where(k == 0, 0.0, jnp.where(k == 1, 0.75, 1.0 / 3.0))
        take = jnp.where(k == 0, 1.0, jnp.where(k == 1, 0.25, 2.0 / 3.0))
        for c in range(2):
            lanes = chunk_lanes(c)
            total = moved[c] + closure[:, lanes].reshape(NF, HALF, LANES)
            fallen = fallv[c, 0, rows8, :]
            total = jnp.concatenate(
                [
                    total[0:3],
                    total[3:4] + heats[rows8, lanes][None],
                    total[4:5],
                    total[5:6] + (tab[6, rows8, lanes] * (fallen - own[c][5]))[None],
                ],
                0,
            )
            sp[k + 1, c + 1, :, rows8, :] = (
                keep * state[:, rows8, lanes] + take * (own[c] + 0.25 * total)
            )

        @pl.when(k < 2)
        def _():
            for copy in halo(k + 1, half):
                copy.start()

            @pl.when(half == 1)
            def _():
                share_levels(k + 1)

        return carry

    lax.fori_loop(0, 6, forward, 0)
    stores = []
    for c in range(2):
        stores.append(
            pltpu.make_async_copy(
                sp.at[3, c + 1], new_state.at[:, :, chunk_lanes(c)], store_sem.at[c]
            )
        )
        stores[-1].start()


    total_rows = nz * share
    scatter = []
    for o in range(1, nz):
        peer = lax.rem(mz + o, nz)
        scatter.append(
            pltpu.make_async_remote_copy(
                src_ref=pack.at[peer], dst_ref=part.at[o],
                send_sem=rs_send.at[o], recv_sem=rs_recv.at[o],
                device_id=(peer, mx), device_id_type=MESH,
            )
        )

    sends_x, receives_x = [], []
    for o in range(1, nx):
        peer, source = lax.rem(mx + o, nx), lax.rem(mx + nx - o, nx)
        for dst, to in ((mx, sends_x), (source, receives_x)):
            to.append(
                pltpu.make_async_remote_copy(
                    src_ref=parts.at[mx], dst_ref=parts.at[dst],
                    send_sem=ag_send.at[o], recv_sem=ag_recv.at[dst],
                    device_id=(mz, peer), device_id_type=MESH,
                )
            )

    def backward(i, carry):
        k = 2 - i
        lam = [lp[i, 0], lp[i, 1]]
        local, masked = [], []
        for c in range(2):
            lanes = chunk_lanes(c)
            source = tab[6, :, lanes] * lam[c][5]
            value = settle(source, lanes, False)
            masked.append(source)
            local.append(value)
            tl[i, mz, 0:levels, lanes] = lam[c][3]
            tl[i, mz, levels:, lanes] = jnp.broadcast_to(value[levels - 1 : levels], (8, LANES))
            for half in range(2):
                out_cot[half, :, lanes] = (
                    lam[c][:, half * HALF : (half + 1) * HALF, :]
                    .reshape(NF * HALF, LANES).astype(BF16)
                )
        sends, receives = level_copies(tl, 1, i)
        for copy in sends:
            copy.start()

        def by_half(half, outer):
            rows8 = rows_of(half)

            def layers(group, inner):
                block = pl.ds(pl.multiple_of(group * (HALF * hid), HALF * hid), HALF * hid)
                first = half * (HALF * hid) + group * (HALF * hid)
                kept = pl.ds(pl.multiple_of(first, HALF * hid), HALF * hid)
                t2 = t2s[k, kept, :]
                t1 = t1s[k, kept, :]
                middle = wmt[...]
                p2 = (mm(k2t[block, :], out_cot[half]) * (1.0 - t2 * t2)).astype(BF16)
                p1 = []
                for j in range(HALF):
                    part_rows = slice(j * hid, (j + 1) * hid)
                    back = mm(middle, p2[part_rows])
                    p1.append((back * (1.0 - t1[part_rows] * t1[part_rows])).astype(BF16))
                pre2[kept, :] = p2
                for j in range(HALF):
                    rows = pl.ds(pl.multiple_of(first + j * hid, hid), hid)
                    pre1[rows, :] = p1[j]
                return inner

            layers(0, 0)
            half_cells = pl.ds(pl.multiple_of(half * (HALF * hid), HALF * hid), HALF * hid)
            feature_cot = mm(k1t[...], pre1[half_cells, :])
            for c in range(2):
                lanes = chunk_lanes(c)
                fcs[c, :, rows8, :] = feature_cot[0 : NF * HALF, lanes].reshape(NF, HALF, LANES)
                now = lp[i, c, :, rows8, :]
                source = (
                    feature_cot[NF * HALF :, lanes].reshape(NF, HALF, LANES)
                    - sp[k, c + 1, 0:1, rows8, :] * now
                )
                gp[c, :, rows8, :] = source
                turned = pltpu.roll(source, NY, 2)
                spread_lam = 0.1 * pltpu.roll(now, NY, 2)
                if c == 0:
                    near = (source - 8.0 * turned) * (1.0 / 12.0) + spread_lam
                    rim_out[i, 0, :, rows8, :] = jnp.where(low, source * (1.0 / 12.0), near)
                else:
                    near = (8.0 * turned - source) * (1.0 / 12.0) + spread_lam
                    rim_out[i, 1, :, rows8, :] = jnp.where(low, near, source * (-1.0 / 12.0))
            for copy in rims(i, half):
                copy.start()
            few = pl.ds(pl.multiple_of(half * (HALF * 16), HALF * 16), HALF * 16)
            by_in[few, :] = mm(pick_in[...], feats[k, half]).astype(BF16)
            by_out[few, :] = mm(pick_out[...], out_cot[half]).astype(BF16)
            return outer

        lax.fori_loop(0, 2, by_half, 0)

        def terms(group, inner):
            s_in, s_out, s_mid = inner
            for j in range(4):
                z = group * 4 + j
                rows = pl.ds(pl.multiple_of(z * hid, hid), hid)
                few = pl.ds(pl.multiple_of(z * 16, 16), 16)
                s_mid = s_mid + mm_t(pre2[rows, :], h1s[k, rows, :])
                s_in = s_in + mm_t(by_in[few, :], pre1[rows, :])
                s_out = s_out + mm_t(by_out[few, :], h2s[k, rows, :])
            return s_in, s_out, s_mid

        s_in, s_out, s_mid = lax.fori_loop(
            0, levels // 4, terms, (a_in[...], a_out[...], a_mid[...])
        )
        a_in[...] = s_in
        a_out[...] = s_out
        a_mid[...] = s_mid

        @pl.when(k == 0)
        def _():
            everything = jnp.concatenate(
                [
                    a_mid[...],
                    a_in[...],
                    a_out[0:8, :],
                    jnp.zeros((total_rows - hid - 24, LANES), F32),
                ],
                0,
            )
            pack[...] = everything.reshape(nz, share, LANES)
            for copy in scatter:
                copy.start()

        for copy in receives:
            copy.wait_recv()
        heat = mm(
            radt[pl.ds(pl.multiple_of(mz * levels, levels), levels), :],
            tl[i, :, 0:levels, :].reshape(nz * levels, columns),
            lax.Precision.HIGHEST,
        )
        zero = jnp.zeros((NF, levels, LANES), F32)
        lam_sides = along_x([zero, lam[0], lam[1], zero])
        g_sides = along_x([zero, gp[0], gp[1], zero])
        weight = jnp.where(k == 0, 1.0, jnp.where(k == 1, 0.0, 0.75))
        share_on = jnp.where(k == 2, 0.25, 1.0)
        wholes = []
        for c in range(2):
            lanes = chunk_lanes(c)
            now = lam[c]
            y_plus, y_minus = along_y(now)
            x_plus, x_minus, _ = lam_sides[c]
            carried_plus, carried_minus = along_y(sp[k, c + 1, 1:2] * now)
            back = (
                (carried_plus - carried_minus) * 0.5
                - g_sides[c][2]
                + 0.1 * (x_plus + x_minus + y_plus + y_minus - 4.0 * now)
                + fcs[c]
            )
            pulled = local[c] + tab[8, :, lanes] * inflow(tl, i, lanes, False)
            back = jnp.concatenate(
                [
                    back[0:1] - jnp.sum(now * dxs[k, c], axis=0, keepdims=True),
                    back[1:2] - jnp.sum(now * dys[k, c], axis=0, keepdims=True),
                    back[2:3],
                    back[3:4] + heat[:, lanes][None],
                    back[4:5],
                    back[5:6] + (pulled - masked[c])[None],
                ],
                0,
            )
            wholes.append(now + 0.25 * back)

        @pl.when(k == 0)
        def _():
            mine = pack[mz]
            for o in range(1, nz):
                scatter[o - 1].wait_recv()
                mine = mine + part[o]
            parts[mx] = mine
            for copy in sends_x:
                copy.start()

        for half in range(2):
            for copy in rims(i, half):
                copy.wait_recv()
        for c in range(2):
            whole = wholes[c] + 0.25 * rim_in[i, c]
            acc[c] = acc[c] + weight * whole
            lp[i + 1, c] = share_on * whole
        return carry

    lax.fori_loop(0, 3, backward, 0)
    for c in range(2):
        stores.append(
            pltpu.make_async_copy(
                acc.at[c], state_grad.at[:, :, chunk_lanes(c)], store_sem.at[2 + c]
            )
        )
        stores[-1].start()

    for copy in receives_x:
        copy.wait_recv()
    summed = parts[0]
    for j in range(1, nx):
        summed = summed + parts[j]

    def quarter(index):
        return pl.ds(pl.multiple_of(index * share, 8), share)

    full[quarter(mz), :] = 0.25 * summed

    sends_z, receives_z = [], []
    for o in range(1, nz):
        peer, source = lax.rem(mz + o, nz), lax.rem(mz + nz - o, nz)
        for dst, to in ((mz, sends_z), (source, receives_z)):
            to.append(
                pltpu.make_async_remote_copy(
                    src_ref=full.at[quarter(mz)], dst_ref=full.at[quarter(dst)],
                    send_sem=fin_send.at[o], recv_sem=fin_recv.at[dst],
                    device_id=(peer, mx), device_id_type=MESH,
                )
            )
    for copy in sends_z:
        copy.start()
    for copy in receives_z:
        copy.wait_recv()
    for at, (out, first, count) in enumerate(
        ((g_mid, 0, hid), (g_in, hid, 2 * NF), (g_out, hid + 16, NF))
    ):
        stores.append(
            pltpu.make_async_copy(full.at[first : first + count], out, store_sem.at[4 + at])
        )
        stores[-1].start()
    for copy in stores:
        copy.wait()
    for k in range(3):
        for half in range(2):
            for copy in halo(k, half) + rims(k, half):
                copy.wait_send()
        for copy in level_copies(tg, 0, k)[0] + level_copies(tl, 1, k)[0]:
            copy.wait_send()
    for copy in scatter + sends_x + sends_z:
        copy.wait_send()


def write_out(*refs):
    sources, outs, held, sems = refs[:5], refs[5:10], refs[10:15], refs[15]
    loads = [pltpu.make_async_copy(sources[at], held[at], sems.at[0, at]) for at in range(5)]
    stores = [pltpu.make_async_copy(held[at], outs[at], sems.at[1, at]) for at in range(5)]
    for copy in loads:
        copy.start()
    for load, store in zip(loads, stores):
        load.wait()
        store.start()
    for copy in stores:
        copy.wait()


def on_device(nz, nx, state, state_cot, w_in, w_mid, w_out, radiation, fall_rate, active):
    fields, levels, columns = state.shape
    hid = w_in.shape[0]
    assert fields == NF and columns == 2 * LANES and hid == LANES and levels == 16
    share = -(-(hid + 24) // (8 * nz)) * 8
    cells = levels * hid
    wide = NF * HALF
    chunk = (4, NF, levels, LANES)
    two = (2, NF, levels, LANES)
    dma = pltpu.SemaphoreType.DMA
    vmem = pltpu.VMEM
    scratch = [
        vmem(state.shape, F32),
        vmem(state.shape, F32),
        vmem((2 * NF, hid), BF16),
        vmem((hid, hid), BF16),
        vmem((NF, hid), BF16),
        vmem(radiation.shape, F32),
        vmem((1, columns), F32),
        vmem((1, columns), active.dtype),
        vmem((HALF * 16, 2 * wide), BF16),
        vmem((HALF * 16, wide), BF16),
        vmem((4,) + chunk, F32),
        vmem((4,) + two, F32),
        vmem(two, F32),
        vmem((3,) + two, F32),
        vmem((3,) + two, F32),
        vmem((2, 1, levels, LANES), F32),
        vmem((levels, columns), F32),
        vmem((3, nz, levels + 8, columns), F32),
        vmem((3, nz, levels + 8, columns), F32),
        vmem((3,) + two, F32),
        vmem((3,) + two, F32),
        vmem((2, NF, HALF, LANES), F32),
        vmem((3, 2, 2 * wide, columns), BF16),
        vmem((2, wide, columns), BF16),
        vmem((3, cells, columns), F32),
        vmem((3, cells, columns), F32),
        vmem((3, cells, columns), BF16),
        vmem((3, cells, columns), BF16),
        vmem((cells // 2, 2 * wide), BF16),
        vmem((2 * wide, cells // 2), BF16),
        vmem((wide, cells // 2), BF16),
        vmem((cells // 2, wide), BF16),
        vmem((hid, hid), BF16),
        vmem((cells, columns), BF16),
        vmem((cells, columns), BF16),
        vmem((levels * 16, columns), BF16),
        vmem((levels * 16, columns), BF16),
        vmem(radiation.shape, F32),
        vmem((9, levels, columns), F32),
        vmem(two, F32),
        vmem(two, F32),
        vmem((16, hid), F32),
        vmem((16, hid), F32),
        vmem((hid, hid), F32),
        vmem((nz, share, LANES), F32),
        vmem((nz, share, LANES), F32),
        vmem((nx, share, LANES), F32),
        vmem((nz * share, LANES), F32),
        dma((8,)), dma((7,)),
        dma((2, 3, 2, 2)), dma((2, 3, 2, 2)),
        dma((2, 3, nz)), dma((2, 3, nz)),
        dma((nz,)), dma((nz,)),
        dma((nx,)), dma((nx,)),
        dma((nz,)), dma((nz,)),
    ]
    results = pl.pallas_call(
        functools.partial(kernel, nz, nx, levels, hid, share),
        out_shape=(
            jax.ShapeDtypeStruct(state.shape, F32),
            jax.ShapeDtypeStruct(state.shape, F32),
            jax.ShapeDtypeStruct((hid, hid), F32),
            jax.ShapeDtypeStruct((2 * NF, hid), F32),
            jax.ShapeDtypeStruct((NF, hid), F32),
        ),
        in_specs=[pl.BlockSpec(memory_space=pl.ANY)] * 8,
        out_specs=[pl.BlockSpec(memory_space=pl.ANY)] * 5,
        scratch_shapes=scratch,
        compiler_params=pltpu.CompilerParams(
            collective_id=0, has_side_effects=True, vmem_limit_bytes=56 * 1024 * 1024
        ),
        name="adjoint_step",
    )(
        state, state_cot, w_in.T, w_mid, w_out, radiation,
        fall_rate.reshape(1, columns), active.reshape(1, columns),
    )
    new_state, state_grad, g_mid, g_in, g_out = pl.pallas_call(
        write_out,
        out_shape=tuple(jax.ShapeDtypeStruct(r.shape, r.dtype) for r in results),
        in_specs=[pl.BlockSpec(memory_space=pl.ANY)] * 5,
        out_specs=[pl.BlockSpec(memory_space=pl.ANY)] * 5,
        scratch_shapes=[vmem(r.shape, r.dtype) for r in results] + [dma((2, 5))],
        compiler_params=pltpu.CompilerParams(vmem_limit_bytes=56 * 1024 * 1024),
        name="write_out",
    )(*results)
    return new_state, state_grad, g_in.T, g_mid, g_out


def solution(mesh):
    placed = (P(None, "gz", "gx"), P(None, "gz", "gx"), P(), P(), P(), P(), P("gx"), P("gx"))
    return jax.shard_map(
        functools.partial(on_device, mesh.shape["gz"], mesh.shape["gx"]),
        mesh=mesh,
        in_specs=placed,
        out_specs=(P(None, "gz", "gx"), P(None, "gz", "gx"), P(), P(), P()),
        check_vma=False,
    )
```

```python
import functools

import jax
import jax.numpy as jnp
from jax import lax
from jax.experimental import pallas as pl
from jax.experimental.pallas import tpu as pltpu
from jax.sharding import PartitionSpec as P

NF = 6
NY = 64
LANES = 128
HALF = 8
HALF_BITS = 3
MESH = pl.DeviceIdType.MESH
F32 = jnp.float32
BF16 = jnp.bfloat16


def mm(a, b, precision=None):
    return lax.dot_general(
        a, b, (((1,), (0,)), ((), ())), precision=precision, preferred_element_type=F32
    )


def mm_t(a, b, precision=None):
    return lax.dot_general(
        a, b, (((1,), (1,)), ((), ())), precision=precision, preferred_element_type=F32
    )


def iota(shape, dim):
    return lax.broadcasted_iota(jnp.int32, shape, dim)


def kernel(
    nz, nx, levels, hid, share,
    state_hbm, cot_hbm, w_in_hbm, w_mid_hbm, w_out_hbm, rad_hbm, fall_hbm, act_hbm,
    new_state, state_grad, g_mid, g_in, g_out,
    state, cot, w_in, w_mid, w_out, rad, fall, act, pick_in, pick_out,
    sp, lp, gp, rim_out, rim_in, fallv, heats, tg, tl, dxs, dys, moved, feats, out_cot, t1s, t2s, h1s, h2s,
    k1, k1t, k2, k2t, wmt, pre1, pre2, by_in, by_out, radt, tab, fcs, acc, a_in, a_out, a_mid,
    pack, part, parts, full,
    load_sem, store_sem, halo_send, halo_recv, gz_send, gz_recv, rs_send, rs_recv, ag_send, ag_recv, fin_send, fin_recv,
):
    mz, mx = lax.axis_index("gz"), lax.axis_index("gx")
    left, right = lax.rem(mx + nx - 1, nx), lax.rem(mx + 1, nx)

    barrier = pltpu.get_barrier_semaphore()
    for o in range(1, nz):
        pl.semaphore_signal(
            barrier, inc=1, device_id=(lax.rem(mz + o, nz), mx), device_id_type=MESH
        )
    for o in range(1, nx):
        pl.semaphore_signal(
            barrier, inc=1, device_id=(mz, lax.rem(mx + o, nx)), device_id_type=MESH
        )

    loads = [
        pltpu.make_async_copy(src, dst, load_sem.at[at])
        for at, (src, dst) in enumerate(
            [
                (state_hbm, state), (cot_hbm, cot), (w_in_hbm, w_in), (w_mid_hbm, w_mid),
                (w_out_hbm, w_out), (rad_hbm, rad), (fall_hbm, fall), (act_hbm, act),
            ]
        )
    ]
    for copy in loads:
        copy.start()
    a_in[...] = jnp.zeros_like(a_in)
    a_out[...] = jnp.zeros_like(a_out)
    a_mid[...] = jnp.zeros_like(a_mid)
    for copy in loads:
        copy.wait()

    columns = 2 * LANES
    shape = (levels, columns)
    rate = jnp.broadcast_to(fall[...], shape)
    r1 = rate / (1.0 + rate)
    r2 = r1 * r1
    r4 = r2 * r2
    r8 = r4 * r4
    powers = [r1, r2, r4, r8, r8 * r8]
    up, down = jnp.ones(shape, F32), jnp.ones(shape, F32)
    level = iota(shape, 0)
    for bit in range(5):
        up = jnp.where(((level + 1) >> bit) & 1 == 1, up * powers[bit], up)
        down = jnp.where(((levels - level) >> bit) & 1 == 1, down * powers[bit], down)
    for at, value in enumerate(
        powers + [1.0 / (1.0 + rate), jnp.broadcast_to(act[...].astype(F32), shape), down, up]
    ):
        tab[at] = value

    for c in range(2):
        lanes = slice(c * LANES, (c + 1) * LANES)
        sp[0, c + 1] = state[:, :, lanes]
        lp[0, c] = (2.0 / 3.0) * cot[:, :, lanes]
        acc[c] = cot[:, :, lanes] * (1.0 / 3.0)

    def rows_of(half):
        return pl.ds(pl.multiple_of(half * HALF, HALF), HALF)

    def sides(sources, targets, kind, k, half):
        return [
            pltpu.make_async_remote_copy(
                src_ref=sources[side].at[:, rows_of(half), :],
                dst_ref=targets[side].at[:, rows_of(half), :],
                send_sem=halo_send.at[kind, k, half, side],
                recv_sem=halo_recv.at[kind, k, half, side],
                device_id=(mz, (left, right)[side]), device_id_type=MESH,
            )
            for side in range(2)
        ]

    def halo(k, half):
        return sides((sp.at[k, 1], sp.at[k, 2]), (sp.at[k, 3], sp.at[k, 0]), 0, k, half)

    def rims(i, half):
        return sides((rim_out.at[i, 0], rim_out.at[i, 1]), (rim_in.at[i, 1], rim_in.at[i, 0]), 1, i, half)

    pl.semaphore_wait(barrier, nz - 1 + nx - 1)
    for half in range(2):
        for copy in halo(0, half):
            copy.start()

    def level_copies(buf, kind, k):
        sends, receives = [], []
        for o in range(1, nz):
            peer, source = lax.rem(mz + o, nz), lax.rem(mz + nz - o, nz)
            for dst, to in ((mz, sends), (source, receives)):
                to.append(
                    pltpu.make_async_remote_copy(
                        src_ref=buf.at[k, mz], dst_ref=buf.at[k, dst],
                        send_sem=gz_send.at[kind, k, o], recv_sem=gz_recv.at[kind, k, dst],
                        device_id=(peer, mx), device_id_type=MESH,
                    )
                )
        return sends, receives

    lane = iota((1, 1, LANES), 2)
    low = lane < NY
    y_last, y_first = lane & (NY - 1) == NY - 1, lane & (NY - 1) == 0
    depth = iota((levels, LANES), 0)

    def along_x(chunks):
        turned = [pltpu.roll(chunk, NY, 2) for chunk in chunks]
        out = []
        for i in (1, 2):
            plus = jnp.where(low, turned[i], turned[i + 1])
            minus = jnp.where(low, turned[i - 1], turned[i])
            out.append((plus, minus, (8.0 * (plus - minus) - (chunks[i + 1] - chunks[i - 1])) * (1.0 / 12.0)))
        return out

    def along_y(chunk):
        plus = jnp.where(y_last, pltpu.roll(chunk, NY - 1, 2), pltpu.roll(chunk, LANES - 1, 2))
        minus = jnp.where(y_first, pltpu.roll(chunk, NY + 1, 2), pltpu.roll(chunk, 1, 2))
        return plus, minus

    def settle(source, lanes, downward):
        value = tab[5, :, lanes] * source
        for bit in range(4):
            step = 1 << bit
            if downward:
                moved_by = pltpu.roll(value, levels - step, 0)
                inside = depth < levels - step
            else:
                moved_by = pltpu.roll(value, step, 0)
                inside = depth >= step
            value = value + tab[bit, :, lanes] * jnp.where(inside, moved_by, 0.0)
        return value

    def inflow(buf, k, lanes, downward):
        total = jnp.zeros((8, LANES), F32)
        order = range(nz - 1, 0, -1) if downward else range(nz - 1)
        for j in order:
            reached = j > mz if downward else j < mz
            following = buf[k, j, levels:, lanes] + tab[4, 0:8, lanes] * total
            total = jnp.where(reached, following, total)
        return total[0:1]

    def chunk_lanes(c):
        return slice(c * LANES, (c + 1) * LANES)

    def share_levels(k):
        for c in range(2):
            lanes = chunk_lanes(c)
            value = settle(sp[k, c + 1, 5], lanes, True)
            fallv[c, 0] = value
            tg[k, mz, 0:levels, lanes] = sp[k, c + 1, 3]
            tg[k, mz, levels:, lanes] = jnp.broadcast_to(value[0:1], (8, LANES))
        for copy in level_copies(tg, 0, k)[0]:
            copy.start()

    share_levels(0)

    def spread_t(rows, cols):
        return (iota((rows, cols), 0) >> HALF_BITS == iota((rows, cols), 1)).astype(F32).astype(BF16)

    eye = (iota((hid, hid), 0) == iota((hid, hid), 1)).astype(F32).astype(BF16)
    w1t = mm(spread_t(2 * NF * HALF, 2 * NF), w_in[...])
    w1 = mm_t(eye, w1t.astype(BF16))
    w2 = mm(spread_t(NF * HALF, NF), w_out[...])
    w2t = mm_t(eye, w2.astype(BF16))
    wmt[...] = mm_t(eye, w_mid[...]).astype(BF16)

    def place(z, carry):
        rows = pl.ds(pl.multiple_of(z * hid, hid), hid)
        k1[rows, :] = jnp.where(iota(w1.shape, 1) & (HALF - 1) == z, w1, 0.0).astype(BF16)
        k2t[rows, :] = jnp.where(iota(w2t.shape, 1) & (HALF - 1) == z, w2t, 0.0).astype(BF16)
        k1t[:, rows] = jnp.where(iota(w1t.shape, 0) & (HALF - 1) == z, w1t, 0.0).astype(BF16)
        k2[:, rows] = jnp.where(iota(w2.shape, 0) & (HALF - 1) == z, w2, 0.0).astype(BF16)
        return carry

    lax.fori_loop(0, HALF, place, 0)
    radt[...] = rad[...].T

    def gathered(cols):
        at = iota((HALF * 16, cols), 0)
        return ((at & 15) * HALF + (at >> 4) == iota((HALF * 16, cols), 1)).astype(F32).astype(BF16)

    pick_in[...] = gathered(2 * NF * HALF)
    pick_out[...] = gathered(NF * HALF)


    def forward(t, carry):
        k, half = t >> 1, t & 1
        rows8 = rows_of(half)
        own = [sp[k, 1, :, rows8, :], sp[k, 2, :, rows8, :]]
        y_sides = [along_y(chunk) for chunk in own]
        carried, spread_y = [], []
        for c in range(2):
            y_plus, y_minus = y_sides[c]
            deriv_y = (y_plus - y_minus) * 0.5
            dys[k, c, :, rows8, :] = deriv_y
            carried.append(own[c][1:2] * deriv_y)
            spread_y.append(y_plus + y_minus - 4.0 * own[c])
            feats[k, half, 0 : NF * HALF, chunk_lanes(c)] = (
                own[c].reshape(NF * HALF, LANES).astype(BF16)
            )
        for copy in halo(k, half):
            copy.wait_recv()
        x_sides = along_x([sp[k, 0, :, rows8, :], own[0], own[1], sp[k, 3, :, rows8, :]])
        for c in range(2):
            x_plus, x_minus, deriv_x = x_sides[c]
            dxs[k, c, :, rows8, :] = deriv_x
            moved[c] = -(own[c][0:1] * deriv_x + carried[c]) + 0.1 * (
                x_plus + x_minus + spread_y[c]
            )
            feats[k, half, NF * HALF :, chunk_lanes(c)] = (
                deriv_x.reshape(NF * HALF, LANES).astype(BF16)
            )

        def layers(group, inner):
            block = pl.ds(pl.multiple_of(group * (HALF * hid), HALF * hid), HALF * hid)
            first = half * (HALF * hid) + group * (HALF * hid)
            kept = pl.ds(pl.multiple_of(first, HALF * hid), HALF * hid)
            middle = w_mid[...]
            t1 = jnp.tanh(mm(k1[block, :], feats[k, half]))
            h1 = t1.astype(BF16)
            t2 = [jnp.tanh(mm(middle, h1[j * hid : (j + 1) * hid])) for j in range(HALF)]
            t1s[k, kept, :] = t1
            h1s[k, kept, :] = h1
            for j in range(HALF):
                rows = pl.ds(pl.multiple_of(first + j * hid, hid), hid)
                t2s[k, rows, :] = t2[j]
                h2s[k, rows, :] = t2[j].astype(BF16)
            return inner

        layers(0, 0)
        half_cells = pl.ds(pl.multiple_of(half * (HALF * hid), HALF * hid), HALF * hid)
        closure = mm(k2[...], h2s[k, half_cells, :])

        @pl.when(half == 0)
        def _():
            for copy in level_copies(tg, 0, k)[1]:
                copy.wait_recv()
            heats[...] = mm(
                rad[pl.ds(pl.multiple_of(mz * levels, levels), levels), :],
                tg[k, :, 0:levels, :].reshape(nz * levels, columns),
                lax.Precision.HIGHEST,
            )
            for c in range(2):
                lanes = chunk_lanes(c)
                fallv[c, 0] = fallv[c, 0] + tab[7, :, lanes] * inflow(tg, k, lanes, True)

        keep = jnp.where(k == 0, 0.0, jnp.where(k == 1, 0.75, 1.0 / 3.0))
        take = jnp.where(k == 0, 1.0, jnp.where(k == 1, 0.25, 2.0 / 3.0))
        for c in range(2):
            lanes = chunk_lanes(c)
            total = moved[c] + closure[:, lanes].reshape(NF, HALF, LANES)
            fallen = fallv[c, 0, rows8, :]
            total = jnp.concatenate(
                [
                    total[0:3],
                    total[3:4] + heats[rows8, lanes][None],
                    total[4:5],
                    total[5:6] + (tab[6, rows8, lanes] * (fallen - own[c][5]))[None],
                ],
                0,
            )
            sp[k + 1, c + 1, :, rows8, :] = (
                keep * state[:, rows8, lanes] + take * (own[c] + 0.25 * total)
            )

        @pl.when(k < 2)
        def _():
            for copy in halo(k + 1, half):
                copy.start()

            @pl.when(half == 1)
            def _():
                share_levels(k + 1)

        return carry

    lax.fori_loop(0, 6, forward, 0)
    stores = []
    for c in range(2):
        stores.append(
            pltpu.make_async_copy(
                sp.at[3, c + 1], new_state.at[:, :, chunk_lanes(c)], store_sem.at[c]
            )
        )
        stores[-1].start()


    total_rows = nz * share
    scatter = []
    for o in range(1, nz):
        peer = lax.rem(mz + o, nz)
        scatter.append(
            pltpu.make_async_remote_copy(
                src_ref=pack.at[peer], dst_ref=part.at[o],
                send_sem=rs_send.at[o], recv_sem=rs_recv.at[o],
                device_id=(peer, mx), device_id_type=MESH,
            )
        )

    sends_x, receives_x = [], []
    for o in range(1, nx):
        peer, source = lax.rem(mx + o, nx), lax.rem(mx + nx - o, nx)
        for dst, to in ((mx, sends_x), (source, receives_x)):
            to.append(
                pltpu.make_async_remote_copy(
                    src_ref=parts.at[mx], dst_ref=parts.at[dst],
                    send_sem=ag_send.at[o], recv_sem=ag_recv.at[dst],
                    device_id=(mz, peer), device_id_type=MESH,
                )
            )

    def backward(i, carry):
        k = 2 - i
        lam = [lp[i, 0], lp[i, 1]]
        local, masked = [], []
        for c in range(2):
            lanes = chunk_lanes(c)
            source = tab[6, :, lanes] * lam[c][5]
            value = settle(source, lanes, False)
            masked.append(source)
            local.append(value)
            tl[i, mz, 0:levels, lanes] = lam[c][3]
            tl[i, mz, levels:, lanes] = jnp.broadcast_to(value[levels - 1 : levels], (8, LANES))
            for half in range(2):
                out_cot[half, :, lanes] = (
                    lam[c][:, half * HALF : (half + 1) * HALF, :]
                    .reshape(NF * HALF, LANES).astype(BF16)
                )
        sends, receives = level_copies(tl, 1, i)
        for copy in sends:
            copy.start()

        def by_half(half, outer):
            rows8 = rows_of(half)

            def layers(group, inner):
                block = pl.ds(pl.multiple_of(group * (HALF * hid), HALF * hid), HALF * hid)
                first = half * (HALF * hid) + group * (HALF * hid)
                kept = pl.ds(pl.multiple_of(first, HALF * hid), HALF * hid)
                t2 = t2s[k, kept, :]
                t1 = t1s[k, kept, :]
                middle = wmt[...]
                p2 = (mm(k2t[block, :], out_cot[half]) * (1.0 - t2 * t2)).astype(BF16)
                p1 = []
                for j in range(HALF):
                    part_rows = slice(j * hid, (j + 1) * hid)
                    back = mm(middle, p2[part_rows])
                    p1.append((back * (1.0 - t1[part_rows] * t1[part_rows])).astype(BF16))
                pre2[kept, :] = p2
                for j in range(HALF):
                    rows = pl.ds(pl.multiple_of(first + j * hid, hid), hid)
                    pre1[rows, :] = p1[j]
                return inner

            layers(0, 0)
            half_cells = pl.ds(pl.multiple_of(half * (HALF * hid), HALF * hid), HALF * hid)
            feature_cot = mm(k1t[...], pre1[half_cells, :])
            for c in range(2):
                lanes = chunk_lanes(c)
                fcs[c, :, rows8, :] = feature_cot[0 : NF * HALF, lanes].reshape(NF, HALF, LANES)
                now = lp[i, c, :, rows8, :]
                source = (
                    feature_cot[NF * HALF :, lanes].reshape(NF, HALF, LANES)
                    - sp[k, c + 1, 0:1, rows8, :] * now
                )
                gp[c, :, rows8, :] = source
                turned = pltpu.roll(source, NY, 2)
                spread_lam = 0.1 * pltpu.roll(now, NY, 2)
                if c == 0:
                    near = (source - 8.0 * turned) * (1.0 / 12.0) + spread_lam
                    rim_out[i, 0, :, rows8, :] = jnp.where(low, source * (1.0 / 12.0), near)
                else:
                    near = (8.0 * turned - source) * (1.0 / 12.0) + spread_lam
                    rim_out[i, 1, :, rows8, :] = jnp.where(low, near, source * (-1.0 / 12.0))
            for copy in rims(i, half):
                copy.start()
            few = pl.ds(pl.multiple_of(half * (HALF * 16), HALF * 16), HALF * 16)
            by_in[few, :] = mm(pick_in[...], feats[k, half]).astype(BF16)
            by_out[few, :] = mm(pick_out[...], out_cot[half]).astype(BF16)
            return outer

        lax.fori_loop(0, 2, by_half, 0)

        def terms(group, inner):
            s_in, s_out, s_mid = inner
            for j in range(HALF):
                z = group * HALF + j
                rows = pl.ds(pl.multiple_of(z * hid, hid), hid)
                few = pl.ds(pl.multiple_of(z * 16, 16), 16)
                s_mid = s_mid + mm_t(pre2[rows, :], h1s[k, rows, :])
                s_in = s_in + mm_t(by_in[few, :], pre1[rows, :])
                s_out = s_out + mm_t(by_out[few, :], h2s[k, rows, :])
            return s_in, s_out, s_mid

        s_in, s_out, s_mid = lax.fori_loop(
            0, levels // HALF, terms, (a_in[...], a_out[...], a_mid[...])
        )
        a_in[...] = s_in
        a_out[...] = s_out
        a_mid[...] = s_mid

        @pl.when(k == 0)
        def _():
            everything = jnp.concatenate(
                [
                    a_mid[...],
                    a_in[...],
                    a_out[0:8, :],
                    jnp.zeros((total_rows - hid - 24, LANES), F32),
                ],
                0,
            )
            pack[...] = everything.reshape(nz, share, LANES)
            for copy in scatter:
                copy.start()

        for copy in receives:
            copy.wait_recv()
        heat = mm(
            radt[pl.ds(pl.multiple_of(mz * levels, levels), levels), :],
            tl[i, :, 0:levels, :].reshape(nz * levels, columns),
            lax.Precision.HIGHEST,
        )
        zero = jnp.zeros((NF, levels, LANES), F32)
        lam_sides = along_x([zero, lam[0], lam[1], zero])
        g_sides = along_x([zero, gp[0], gp[1], zero])
        weight = jnp.where(k == 0, 1.0, jnp.where(k == 1, 0.0, 0.75))
        share_on = jnp.where(k == 2, 0.25, 1.0)
        wholes = []
        for c in range(2):
            lanes = chunk_lanes(c)
            now = lam[c]
            y_plus, y_minus = along_y(now)
            x_plus, x_minus, _ = lam_sides[c]
            carried_plus, carried_minus = along_y(sp[k, c + 1, 1:2] * now)
            back = (
                (carried_plus - carried_minus) * 0.5
                - g_sides[c][2]
                + 0.1 * (x_plus + x_minus + y_plus + y_minus - 4.0 * now)
                + fcs[c]
            )
            pulled = local[c] + tab[8, :, lanes] * inflow(tl, i, lanes, False)
            back = jnp.concatenate(
                [
                    back[0:1] - jnp.sum(now * dxs[k, c], axis=0, keepdims=True),
                    back[1:2] - jnp.sum(now * dys[k, c], axis=0, keepdims=True),
                    back[2:3],
                    back[3:4] + heat[:, lanes][None],
                    back[4:5],
                    back[5:6] + (pulled - masked[c])[None],
                ],
                0,
            )
            wholes.append(now + 0.25 * back)

        @pl.when(k == 0)
        def _():
            mine = pack[mz]
            for o in range(1, nz):
                scatter[o - 1].wait_recv()
                mine = mine + part[o]
            parts[mx] = mine
            for copy in sends_x:
                copy.start()

        for half in range(2):
            for copy in rims(i, half):
                copy.wait_recv()
        for c in range(2):
            whole = wholes[c] + 0.25 * rim_in[i, c]
            acc[c] = acc[c] + weight * whole
            lp[i + 1, c] = share_on * whole
        return carry

    lax.fori_loop(0, 3, backward, 0)
    for c in range(2):
        stores.append(
            pltpu.make_async_copy(
                acc.at[c], state_grad.at[:, :, chunk_lanes(c)], store_sem.at[2 + c]
            )
        )
        stores[-1].start()

    for copy in receives_x:
        copy.wait_recv()
    summed = parts[0]
    for j in range(1, nx):
        summed = summed + parts[j]

    def quarter(index):
        return pl.ds(pl.multiple_of(index * share, 8), share)

    full[quarter(mz), :] = 0.25 * summed

    sends_z, receives_z = [], []
    for o in range(1, nz):
        peer, source = lax.rem(mz + o, nz), lax.rem(mz + nz - o, nz)
        for dst, to in ((mz, sends_z), (source, receives_z)):
            to.append(
                pltpu.make_async_remote_copy(
                    src_ref=full.at[quarter(mz)], dst_ref=full.at[quarter(dst)],
                    send_sem=fin_send.at[o], recv_sem=fin_recv.at[dst],
                    device_id=(peer, mx), device_id_type=MESH,
                )
            )
    for copy in sends_z:
        copy.start()
    for copy in receives_z:
        copy.wait_recv()
    for at, (out, first, count) in enumerate(
        ((g_mid, 0, hid), (g_in, hid, 2 * NF), (g_out, hid + 16, NF))
    ):
        stores.append(
            pltpu.make_async_copy(full.at[first : first + count], out, store_sem.at[4 + at])
        )
        stores[-1].start()
    for copy in stores:
        copy.wait()
    for k in range(3):
        for half in range(2):
            for copy in halo(k, half) + rims(k, half):
                copy.wait_send()
        for copy in level_copies(tg, 0, k)[0] + level_copies(tl, 1, k)[0]:
            copy.wait_send()
    for copy in scatter + sends_x + sends_z:
        copy.wait_send()


def write_out(*refs):
    sources, outs, held, sems = refs[:5], refs[5:10], refs[10:15], refs[15]
    loads = [pltpu.make_async_copy(sources[at], held[at], sems.at[0, at]) for at in range(5)]
    stores = [pltpu.make_async_copy(held[at], outs[at], sems.at[1, at]) for at in range(5)]
    for copy in loads:
        copy.start()
    for load, store in zip(loads, stores):
        load.wait()
        store.start()
    for copy in stores:
        copy.wait()


def on_device(nz, nx, state, state_cot, w_in, w_mid, w_out, radiation, fall_rate, active):
    fields, levels, columns = state.shape
    hid = w_in.shape[0]
    assert fields == NF and columns == 2 * LANES and hid == LANES and levels == 16
    share = -(-(hid + 24) // (8 * nz)) * 8
    cells = levels * hid
    wide = NF * HALF
    chunk = (4, NF, levels, LANES)
    two = (2, NF, levels, LANES)
    dma = pltpu.SemaphoreType.DMA
    vmem = pltpu.VMEM
    scratch = [
        vmem(state.shape, F32),
        vmem(state.shape, F32),
        vmem((2 * NF, hid), BF16),
        vmem((hid, hid), BF16),
        vmem((NF, hid), BF16),
        vmem(radiation.shape, F32),
        vmem((1, columns), F32),
        vmem((1, columns), active.dtype),
        vmem((HALF * 16, 2 * wide), BF16),
        vmem((HALF * 16, wide), BF16),
        vmem((4,) + chunk, F32),
        vmem((4,) + two, F32),
        vmem(two, F32),
        vmem((3,) + two, F32),
        vmem((3,) + two, F32),
        vmem((2, 1, levels, LANES), F32),
        vmem((levels, columns), F32),
        vmem((3, nz, levels + 8, columns), F32),
        vmem((3, nz, levels + 8, columns), F32),
        vmem((3,) + two, F32),
        vmem((3,) + two, F32),
        vmem((2, NF, HALF, LANES), F32),
        vmem((3, 2, 2 * wide, columns), BF16),
        vmem((2, wide, columns), BF16),
        vmem((3, cells, columns), F32),
        vmem((3, cells, columns), F32),
        vmem((3, cells, columns), BF16),
        vmem((3, cells, columns), BF16),
        vmem((cells // 2, 2 * wide), BF16),
        vmem((2 * wide, cells // 2), BF16),
        vmem((wide, cells // 2), BF16),
        vmem((cells // 2, wide), BF16),
        vmem((hid, hid), BF16),
        vmem((cells, columns), BF16),
        vmem((cells, columns), BF16),
        vmem((levels * 16, columns), BF16),
        vmem((levels * 16, columns), BF16),
        vmem(radiation.shape, F32),
        vmem((9, levels, columns), F32),
        vmem(two, F32),
        vmem(two, F32),
        vmem((16, hid), F32),
        vmem((16, hid), F32),
        vmem((hid, hid), F32),
        vmem((nz, share, LANES), F32),
        vmem((nz, share, LANES), F32),
        vmem((nx, share, LANES), F32),
        vmem((nz * share, LANES), F32),
        dma((8,)), dma((7,)),
        dma((2, 3, 2, 2)), dma((2, 3, 2, 2)),
        dma((2, 3, nz)), dma((2, 3, nz)),
        dma((nz,)), dma((nz,)),
        dma((nx,)), dma((nx,)),
        dma((nz,)), dma((nz,)),
    ]
    results = pl.pallas_call(
        functools.partial(kernel, nz, nx, levels, hid, share),
        out_shape=(
            jax.ShapeDtypeStruct(state.shape, F32),
            jax.ShapeDtypeStruct(state.shape, F32),
            jax.ShapeDtypeStruct((hid, hid), F32),
            jax.ShapeDtypeStruct((2 * NF, hid), F32),
            jax.ShapeDtypeStruct((NF, hid), F32),
        ),
        in_specs=[pl.BlockSpec(memory_space=pl.ANY)] * 8,
        out_specs=[pl.BlockSpec(memory_space=pl.ANY)] * 5,
        scratch_shapes=scratch,
        compiler_params=pltpu.CompilerParams(
            collective_id=0, has_side_effects=True, vmem_limit_bytes=56 * 1024 * 1024
        ),
        name="adjoint_step",
    )(
        state, state_cot, w_in.T, w_mid, w_out, radiation,
        fall_rate.reshape(1, columns), active.reshape(1, columns),
    )
    new_state, state_grad, g_mid, g_in, g_out = pl.pallas_call(
        write_out,
        out_shape=tuple(jax.ShapeDtypeStruct(r.shape, r.dtype) for r in results),
        in_specs=[pl.BlockSpec(memory_space=pl.ANY)] * 5,
        out_specs=[pl.BlockSpec(memory_space=pl.ANY)] * 5,
        scratch_shapes=[vmem(r.shape, r.dtype) for r in results] + [dma((2, 5))],
        compiler_params=pltpu.CompilerParams(vmem_limit_bytes=56 * 1024 * 1024),
        name="write_out",
    )(*results)
    return new_state, state_grad, g_in.T, g_mid, g_out


def solution(mesh):
    placed = (P(None, "gz", "gx"), P(None, "gz", "gx"), P(), P(), P(), P(), P("gx"), P("gx"))
    return jax.shard_map(
        functools.partial(on_device, mesh.shape["gz"], mesh.shape["gx"]),
        mesh=mesh,
        in_specs=placed,
        out_specs=(P(None, "gz", "gx"), P(None, "gz", "gx"), P(), P(), P()),
        check_vma=False,
    )
```
